32 devices in a mesh: groups: 2 (over y), rows: 4 (over z), cols: 2 (over x), sub: 2 (over core).
Axes of the slice: x: 2, y: 2, z: 4, core: 2. Of those that a mesh axis runs over, the one named last changes fastest.
Arguments:
- activations: float32 [2048, 8192], P(('groups', 'rows', 'sub'), 'cols'), parts along dimension 0, may hold values from -72 to 72
- plan: int32 [2, 32], replicated, may hold values from 0 to 31, as said below
Outputs:
- rotated: float32 [2048, 8192], P(('groups', 'rows', 'sub'), 'cols'), parts along dimension 0
The draws below stay inside these ranges and needn't reach their ends.
There are 2 independent parts, one for each index of `groups`. The reference program is written for one: setup_inputs(seed, part) draws one part's arguments, and reference() takes and returns one part's arrays. A program takes and returns all parts, laid end to end along the dimension named above; an argument that names none is the same for every part. Nothing has to cross between parts.
Inputs may be any that keep to these rules, and one draw needn't show every extreme that they name: `plan`: each row is a permutation of the blocks. In row 0 the slots j*16 to (j+1)*16 - 1 hold exactly the blocks numbered j*16 to (j+1)*16 - 1. Row r+1 follows row r by the round-robin move: new slot 0 takes old slot 0, new slot 2 takes old slot 1, new slot 2k (k >= 2) takes old slot 2k-2, new slot 2k+1 takes old slot 2k+3 for k < 15, and new slot 31 takes old slot 30.
All inputs are finite; a program needn't handle non-finite values.
Results may differ from the reference program's by a relative error of at most 0.0014.
Values sent between devices are 32-bit elements; how exact they have to be, the bound alone decides.
No kernel may reach another device: no remote copies, remote signals or barrier semaphores. Data moves between devices by JAX's collectives and lax.ppermute only.
A program may use at most 64 MiB of HBM per device.

```python
import math
import jax
import jax.numpy as jnp
from jax import lax

NCOL = 8192
BLK = 256
ROUNDS = 2
TOKENS = 1024
NBLK = 32
PAIRS = 16
BLK_DEV = 16


def draw_activations(key, part):
    key = jax.random.fold_in(key, 11)
    first, second, third = jax.random.split(key, 3)
    col_scale = jnp.exp(jax.random.uniform(second, (1, NCOL), jnp.float32, math.log(0.3), math.log(3.0)))
    base = jnp.clip(jax.random.normal(first, (TOKENS, NCOL), jnp.float32), -6.0, 6.0)
    row_scale = jnp.exp(jax.random.uniform(third, (TOKENS, 1), jnp.float32, math.log(0.5), math.log(2.0)))
    return (base * col_scale * row_scale).astype(jnp.float32)


def draw_plan(key, part):
    key = jax.random.fold_in(key, 7)
    groups_count = NBLK // BLK_DEV
    keys = jax.random.split(key, groups_count)
    perms = jax.vmap(lambda single: jax.random.permutation(single, BLK_DEV))(keys).astype(jnp.int32)
    offsets = (jnp.arange(groups_count, dtype=jnp.int32) * BLK_DEV)[:, None]
    current = (perms + offsets).reshape(NBLK)
    slots = jnp.arange(NBLK, dtype=jnp.int32)
    pair_of = slots // 2
    upper_src = jnp.where(pair_of == 0, 0, jnp.where(pair_of == 1, 1, 2 * pair_of - 2))
    lower_src = jnp.where(pair_of <= PAIRS - 2, 2 * pair_of + 3, 2 * PAIRS - 2)
    source = jnp.where(slots % 2 == 0, upper_src, lower_src).astype(jnp.int32)
    rows_list = [current]
    for round_index in range(ROUNDS - 1):
        current = current[source]
        rows_list.append(current)
    return jnp.stack(rows_list, axis=0).astype(jnp.int32)


def setup_inputs(seed: int = 0, part: int = 0) -> dict:
    key_of = jax.random.split(jax.random.key(seed), 3)
    part_splits = jax.random.split(jax.random.fold_in(key_of[2], part), 3)
    activations = draw_activations(jax.random.fold_in(jax.random.fold_in(key_of[2], part), 71), part)
    plan = draw_plan(jax.random.fold_in(key_of[2], 71), part)
    return {"activations": activations, "plan": plan}


epsilon = 1e-06

def rotate(cross, upper_sq, lower_sq, upper, lower):
    high = lax.Precision.HIGHEST
    corr = cross * lax.rsqrt(upper_sq + epsilon)[:, :, None] * lax.rsqrt(lower_sq + epsilon)[:, None, :]
    ident = jnp.eye(corr.shape[1], dtype=jnp.float32)
    left_chol = jnp.linalg.cholesky(ident + jnp.einsum('pik,pjk->pij', corr, corr, precision=high))
    right_chol = jnp.linalg.cholesky(ident + jnp.einsum('pki,pkj->pij', corr, corr, precision=high))
    invert = jax.vmap(lambda factor: jax.scipy.linalg.solve_triangular(factor, ident, lower=True))
    left_inv = invert(left_chol)
    right_inv = invert(right_chol)
    mixed_upper = upper + jnp.einsum('tpk,pik->tpi', lower, corr, precision=high)
    mixed_lower = lower - jnp.einsum('tpk,pkj->tpj', upper, corr, precision=high)
    new_upper = jnp.einsum('tpk,pjk->tpj', mixed_upper, left_inv, precision=high)
    new_lower = jnp.einsum('tpk,pjk->tpj', mixed_lower, right_inv, precision=high)
    return (new_upper, new_lower)

def reference(activations, plan):
    high = lax.Precision.HIGHEST
    blocks = activations.reshape(TOKENS, NBLK, BLK)
    slotted = blocks
    for round_index in range(ROUNDS):
        order = plan[round_index].astype(jnp.int32)
        slotted = jnp.take(blocks, order, axis=1)
        upper = slotted[:, 0::2]
        lower = slotted[:, 1::2]
        cross = jnp.einsum('tpi,tpj->pij', upper, lower, precision=high)
        upper_sq = lax.optimization_barrier(jnp.sum(upper * upper, axis=0))
        lower_sq = lax.optimization_barrier(jnp.sum(lower * lower, axis=0))
        new_upper, new_lower = rotate(cross, upper_sq, lower_sq, upper, lower)
        slotted = jnp.stack([new_upper, new_lower], axis=2).reshape(TOKENS, NBLK, BLK)
        if round_index + 1 < ROUNDS:
            blocks = blocks.at[:, order].set(slotted)
    return slotted.reshape(TOKENS, NCOL)
```

```python
import functools

import jax
import jax.numpy as jnp
from jax import lax
from jax.experimental import pallas as pl
from jax.experimental.pallas import tpu as pltpu
from jax.sharding import PartitionSpec as P

BLK = 256
ROUNDS = 2
PANEL = 64
SUBLANES = 8

epsilon = 1e-06
HIGH = lax.Precision.HIGHEST
VMEM_LIMIT = 40 * 1024 * 1024


def contract(a, b, a_dim, b_dim):
    return lax.dot_general(
        a, b, (((a_dim,), (b_dim,)), ((), ())), precision=HIGH, preferred_element_type=jnp.float32
    )


def iota2(shape, dim):
    return lax.broadcasted_iota(jnp.int32, shape, dim)


def eliminate(blocks):
    width = 2 * PANEL
    tiles = PANEL // SUBLANES
    ident = jnp.where(iota2((PANEL, PANEL), 0) == iota2((PANEL, PANEL), 1), 1.0, 0.0).astype(jnp.float32)
    parts = []
    for block in blocks:
        whole = jnp.concatenate([block, ident], axis=1)
        parts.append([whole[SUBLANES * v : SUBLANES * (v + 1)] for v in range(tiles)])
    sub = iota2((SUBLANES, width), 0)
    for j in range(PANEL):
        home, line = divmod(j, SUBLANES)
        for part in parts:
            row = part[home][line : line + 1, :]
            scaled = row / row[:, j : j + 1]
            for v in range(home, tiles):
                column = part[v][:, j : j + 1]
                step = column * scaled
                if v == home:
                    step = jnp.where(sub > line, step, 0.0)
                part[v] = part[v] - step
    outs = []
    on_diagonal = iota2((PANEL, width), 0) == iota2((PANEL, width), 1)
    for part in parts:
        whole = jnp.concatenate(part, axis=0)
        pivots = jnp.sum(jnp.where(on_diagonal, whole, 0.0), axis=1, keepdims=True)
        outs.append(whole[:, PANEL:] * lax.rsqrt(pivots))
    return outs


def inverse_factors(aug_ref):
    for p in range(BLK // PANEL):
        top = p * PANEL
        end = top + PANEL
        blocks = [aug_ref[m, top:end, top:end] for m in range(2)]
        invs = eliminate(blocks)
        for m in range(2):
            rows = contract(invs[m], aug_ref[m, top:end, :], 1, 0)
            aug_ref[m, top:end, BLK:] = rows[:, BLK:]
            if end < BLK:
                aug_ref[m, end:, :] = aug_ref[m, end:, :] - contract(rows[:, end:BLK], rows, 0, 0)


def rotate_pair(upper_ref, lower_ref, cross, upper_sq, lower_sq, aug_ref):
    square = (BLK, BLK)
    diagonal = iota2(square, 0) == iota2(square, 1)
    ident = jnp.where(diagonal, 1.0, 0.0).astype(jnp.float32)
    upper_sq = jnp.sum(
        jnp.where(diagonal, jnp.broadcast_to(upper_sq, square), 0.0), axis=1, keepdims=True
    )
    corr = cross * lax.rsqrt(upper_sq + epsilon) * lax.rsqrt(lower_sq + epsilon)
    aug_ref[0, :, :BLK] = ident + contract(corr, corr, 1, 1)
    aug_ref[1, :, :BLK] = ident + contract(corr, corr, 0, 0)
    aug_ref[0, :, BLK:] = ident
    aug_ref[1, :, BLK:] = ident
    inverse_factors(aug_ref)
    upper = upper_ref[...]
    lower = lower_ref[...]
    mixed_upper = upper + contract(lower, corr, 1, 1)
    mixed_lower = lower - contract(upper, corr, 1, 0)
    new_upper = contract(mixed_upper, aug_ref[0, :, BLK:], 1, 1)
    new_lower = contract(mixed_lower, aug_ref[1, :, BLK:], 1, 1)
    return new_upper, new_lower


def terms_of(upper, lower):
    return (
        contract(upper, lower, 0, 0),
        jnp.sum(upper * upper, axis=0, keepdims=True),
        jnp.sum(lower * lower, axis=0, keepdims=True),
    )


def pack_kernel(order_ref, x_ref, *refs):
    outs, sem = refs[:-1], refs[-1]
    copies = []
    for i, out in enumerate(outs):
        for half in range(2):
            start = pl.multiple_of(order_ref[2 * i + half] * BLK, BLK)
            copies.append(
                pltpu.make_async_copy(
                    x_ref.at[:, pl.ds(start, BLK)],
                    out.at[:, half * BLK : (half + 1) * BLK],
                    sem.at[2 * i + half],
                )
            )
    for copy in copies:
        copy.start()
    for copy in copies:
        copy.wait()


def pack(order, x, count):
    rows = x.shape[0]
    piece = jax.ShapeDtypeStruct((rows, 2 * BLK), jnp.float32)
    return pl.pallas_call(
        pack_kernel,
        out_shape=[piece] * count,
        in_specs=[pl.BlockSpec(memory_space=pltpu.SMEM), pl.BlockSpec(memory_space=pl.ANY)],
        out_specs=[pl.BlockSpec(memory_space=pl.ANY)] * count,
        scratch_shapes=[pltpu.SemaphoreType.DMA((2 * count,))],
        name="pack",
    )(order, x)


def unpack_kernel(place_ref, *refs):
    pieces, out_ref, sem = refs[:-2], refs[-2], refs[-1]
    width = 2 * BLK
    copies = []
    for i, piece in enumerate(pieces):
        start = pl.multiple_of(place_ref[i] * width, width)
        copies.append(pltpu.make_async_copy(piece, out_ref.at[:, pl.ds(start, width)], sem.at[i]))
    for copy in copies:
        copy.start()
    for copy in copies:
        copy.wait()


def unpack(place, pieces):
    rows, width = pieces[0].shape
    count = len(pieces)
    return pl.pallas_call(
        unpack_kernel,
        out_shape=jax.ShapeDtypeStruct((rows, count * width), jnp.float32),
        in_specs=[pl.BlockSpec(memory_space=pltpu.SMEM)]
        + [pl.BlockSpec(memory_space=pl.ANY)] * count,
        out_specs=pl.BlockSpec(memory_space=pl.ANY),
        scratch_shapes=[pltpu.SemaphoreType.DMA((count,))],
        name="unpack",
    )(place, *pieces)


def first_kernel(count, given, source_ref, *refs):
    pieces = refs[:count]
    refs = refs[count:]
    terms, refs = refs[: 3 * given], refs[3 * given :]
    new_upper_ref, new_lower_ref, upper_ref, lower_ref, aug_ref, sem = refs
    rows = pieces[0].shape[0]
    copies = []
    for i, piece in enumerate(pieces):
        start = pl.multiple_of(source_ref[i] * rows, rows)
        for half, target in enumerate((upper_ref, lower_ref)):
            copies.append(
                pltpu.make_async_copy(
                    piece.at[:, half * BLK : (half + 1) * BLK],
                    target.at[pl.ds(start, rows), :],
                    sem.at[2 * i + half],
                )
            )
    for copy in copies:
        copy.start()
    for copy in copies:
        copy.wait()
    if given:
        cross, upper_sq, lower_sq = (term[...] for term in terms)
    else:
        cross, upper_sq, lower_sq = terms_of(upper_ref[...], lower_ref[...])
    new_upper, new_lower = rotate_pair(upper_ref, lower_ref, cross, upper_sq, lower_sq, aug_ref)
    new_upper_ref[...] = new_upper
    new_lower_ref[...] = new_lower


def first_round(source, pieces, terms):
    rows = pieces[0].shape[0]
    count = len(pieces)
    tokens = rows * count
    block = jax.ShapeDtypeStruct((tokens, BLK), jnp.float32)
    vmem = pl.BlockSpec(memory_space=pltpu.VMEM)
    return pl.pallas_call(
        functools.partial(first_kernel, count, int(bool(terms))),
        out_shape=[block, block],
        in_specs=[pl.BlockSpec(memory_space=pltpu.SMEM)]
        + [pl.BlockSpec(memory_space=pl.ANY)] * count
        + [vmem] * len(terms),
        out_specs=[vmem, vmem],
        scratch_shapes=[
            pltpu.VMEM((tokens, BLK), jnp.float32),
            pltpu.VMEM((tokens, BLK), jnp.float32),
            pltpu.VMEM((2, BLK, 2 * BLK), jnp.float32),
            pltpu.SemaphoreType.DMA((2 * count,)),
        ],
        compiler_params=pltpu.CompilerParams(vmem_limit_bytes=VMEM_LIMIT),
        name="first_round",
    )(source, *pieces, *terms)


def last_kernel(count, given, source_ref, upper_ref, lower_ref, *refs):
    terms, refs = refs[: 3 * given], refs[3 * given :]
    outs = refs[:count]
    result_ref, aug_ref, sem = refs[count:]
    rows = outs[0].shape[0]
    if given:
        cross, upper_sq, lower_sq = (term[...] for term in terms)
    else:
        cross, upper_sq, lower_sq = terms_of(upper_ref[...], lower_ref[...])
    new_upper, new_lower = rotate_pair(upper_ref, lower_ref, cross, upper_sq, lower_sq, aug_ref)
    result_ref[:, :BLK] = new_upper
    result_ref[:, BLK:] = new_lower
    copies = []
    for i, out in enumerate(outs):
        start = pl.multiple_of(source_ref[i] * rows, rows)
        copies.append(pltpu.make_async_copy(result_ref.at[pl.ds(start, rows), :], out, sem.at[i]))
    for copy in copies:
        copy.start()
    for copy in copies:
        copy.wait()


def last_round(source, upper, lower, terms):
    tokens = upper.shape[0]
    count = source.shape[0]
    piece = jax.ShapeDtypeStruct((tokens // count, 2 * BLK), jnp.float32)
    vmem = pl.BlockSpec(memory_space=pltpu.VMEM)
    return pl.pallas_call(
        functools.partial(last_kernel, count, int(bool(terms))),
        out_shape=[piece] * count,
        in_specs=[pl.BlockSpec(memory_space=pltpu.SMEM), vmem, vmem] + [vmem] * len(terms),
        out_specs=[pl.BlockSpec(memory_space=pl.ANY)] * count,
        scratch_shapes=[
            pltpu.VMEM((tokens, 2 * BLK), jnp.float32),
            pltpu.VMEM((2, BLK, 2 * BLK), jnp.float32),
            pltpu.SemaphoreType.DMA((count,)),
        ],
        compiler_params=pltpu.CompilerParams(vmem_limit_bytes=VMEM_LIMIT),
        name="last_round",
    )(source, upper, lower, *terms)


def on_device(activations, plan):
    token_axes = ("rows", "sub")
    all_axes = ("rows", "cols", "sub")
    subs = lax.axis_size("sub")
    columns = lax.axis_size("cols")
    column = lax.axis_index("cols")
    block_count = activations.shape[1] // BLK
    pairs = block_count // 2
    token_group = lax.axis_size(token_axes)
    token_index = lax.axis_index(token_axes)
    teams = token_group // pairs
    assert teams * pairs == token_group and pairs & (pairs - 1) == 0
    member = token_index % pairs
    shifts = jnp.arange(pairs, dtype=jnp.int32)
    partner = jnp.bitwise_xor(member, shifts)
    backwards = column % 2 == 1

    def pair_of(member):
        return jnp.where(backwards, pairs - 1 - member, member)

    def exchange(pieces):
        arrived = [pieces[0]]
        for shift in range(1, pairs):
            route = [(t, t ^ shift) for t in range(token_group)]
            arrived.append(lax.ppermute(pieces[shift], token_axes, route))
        return arrived

    def added_up(upper, lower):
        groups = [[team * pairs + m for team in range(teams)] for m in range(pairs)]
        total = []
        for term in terms_of(upper, lower):
            full = term
            for step in range(1, teams):
                route = [
                    (group[i], group[(i + step) % teams]) for group in groups for i in range(teams)
                ]
                full = full + lax.ppermute(term, token_axes, route)
            total.append(full)
        return total

    local_order = (
        lax.dynamic_slice_in_dim(plan[0], column * block_count, block_count) - column * block_count
    )
    order = jnp.take(local_order.reshape(pairs, 2), pair_of(partner), axis=0).reshape(-1)
    pieces = exchange(pack(order, activations, pairs))

    terms = []
    if teams > 1:
        canonical = jnp.concatenate(pieces, axis=0)
        terms = added_up(canonical[:, :BLK], canonical[:, BLK:])
    upper, lower = first_round(partner, pieces, terms)

    def device_of(pair):
        home, inner = divmod(pair, pairs)
        return home, pairs - 1 - inner if home % 2 else inner

    total_pairs = columns * pairs
    chain = column * pairs + pair_of(member)
    first = chain == 0
    final = chain == total_pairs - 1

    def along(block, distance):
        route = []
        for pair in range(total_pairs):
            if 0 <= pair + distance < total_pairs:
                for team in range(teams):
                    ends = []
                    for one in (pair, pair + distance):
                        home, inner = device_of(one)
                        row, sub = divmod(team * pairs + inner, subs)
                        ends.append((row * columns + home) * subs + sub)
                    route.append(tuple(ends))
        return lax.ppermute(block, all_axes, route)

    arriving = along(jnp.where(first, lower, upper), 1)
    leaving = along(lower, -1)
    next_upper = jnp.where(first, upper, arriving)
    next_lower = jnp.where(final, upper, leaving)

    terms = added_up(next_upper, next_lower) if teams > 1 else []
    pieces = exchange(last_round(partner, next_upper, next_lower, terms))
    return unpack(pair_of(partner), pieces)


def solution(mesh):
    in_specs = (P(("groups", "rows", "sub"), "cols"), P())
    out_specs = P(("groups", "rows", "sub"), "cols")
    return jax.shard_map(
        on_device, mesh=mesh, in_specs=in_specs, out_specs=out_specs, check_vma=False
    )
```

```python
import functools

import jax
import jax.numpy as jnp
from jax import lax
from jax.experimental import pallas as pl
from jax.experimental.pallas import tpu as pltpu
from jax.sharding import PartitionSpec as P

BLK = 256
ROUNDS = 2
PANEL = 64
SUBLANES = 8

epsilon = 1e-06
HIGH = lax.Precision.HIGHEST
VMEM_LIMIT = 40 * 1024 * 1024


def contract(a, b, a_dim, b_dim):
    return lax.dot_general(
        a, b, (((a_dim,), (b_dim,)), ((), ())), precision=HIGH, preferred_element_type=jnp.float32
    )


def iota2(shape, dim):
    return lax.broadcasted_iota(jnp.int32, shape, dim)


def eliminate(blocks):
    width = 2 * PANEL
    tiles = PANEL // SUBLANES
    ident = jnp.where(iota2((PANEL, PANEL), 0) == iota2((PANEL, PANEL), 1), 1.0, 0.0).astype(jnp.float32)
    parts = []
    for block in blocks:
        whole = jnp.concatenate([block, ident], axis=1)
        parts.append([whole[SUBLANES * v : SUBLANES * (v + 1)] for v in range(tiles)])
    sub = iota2((SUBLANES, width), 0)
    for j in range(PANEL):
        home, line = divmod(j, SUBLANES)
        for part in parts:
            row = part[home][line : line + 1, :]
            scaled = row / row[:, j : j + 1]
            for v in range(home, tiles):
                column = part[v][:, j : j + 1]
                step = column * scaled
                if v == home:
                    step = jnp.where(sub > line, step, 0.0)
                part[v] = part[v] - step
    outs = []
    on_diagonal = iota2((PANEL, width), 0) == iota2((PANEL, width), 1)
    for part in parts:
        whole = jnp.concatenate(part, axis=0)
        pivots = jnp.sum(jnp.where(on_diagonal, whole, 0.0), axis=1, keepdims=True)
        outs.append(whole[:, PANEL:] * lax.rsqrt(pivots))
    return outs


def inverse_factors(aug_ref):
    for p in range(BLK // PANEL):
        top = p * PANEL
        end = top + PANEL
        blocks = [aug_ref[m, top:end, top:end] for m in range(2)]
        invs = eliminate(blocks)
        for m in range(2):
            rows = contract(invs[m], aug_ref[m, top:end, :], 1, 0)
            aug_ref[m, top:end, BLK:] = rows[:, BLK:]
            if end < BLK:
                aug_ref[m, end:, :] = aug_ref[m, end:, :] - contract(rows[:, end:BLK], rows, 0, 0)


def rotate_pair(upper_ref, lower_ref, cross, upper_sq, lower_sq, aug_ref):
    square = (BLK, BLK)
    diagonal = iota2(square, 0) == iota2(square, 1)
    ident = jnp.where(diagonal, 1.0, 0.0).astype(jnp.float32)
    upper_sq = jnp.sum(
        jnp.where(diagonal, jnp.broadcast_to(upper_sq, square), 0.0), axis=1, keepdims=True
    )
    corr = cross * lax.rsqrt(upper_sq + epsilon) * lax.rsqrt(lower_sq + epsilon)
    aug_ref[0, :, :BLK] = ident + contract(corr, corr, 1, 1)
    aug_ref[1, :, :BLK] = ident + contract(corr, corr, 0, 0)
    aug_ref[0, :, BLK:] = ident
    aug_ref[1, :, BLK:] = ident
    inverse_factors(aug_ref)
    upper = upper_ref[...]
    lower = lower_ref[...]
    mixed_upper = upper + contract(lower, corr, 1, 1)
    mixed_lower = lower - contract(upper, corr, 1, 0)
    new_upper = contract(mixed_upper, aug_ref[0, :, BLK:], 1, 1)
    new_lower = contract(mixed_lower, aug_ref[1, :, BLK:], 1, 1)
    return new_upper, new_lower


def terms_of(upper, lower):
    return (
        contract(upper, lower, 0, 0),
        jnp.sum(upper * upper, axis=0, keepdims=True),
        jnp.sum(lower * lower, axis=0, keepdims=True),
    )


def pack_kernel(order_ref, x_ref, *refs):
    outs, held, in_sem, out_sem = refs[:-3], *refs[-3:]
    count = len(outs)
    loads, stores = [], []
    for i, out in enumerate(outs):
        for half in range(2):
            start = pl.multiple_of(order_ref[2 * i + half] * BLK, BLK)
            loads.append(
                pltpu.make_async_copy(
                    x_ref.at[:, pl.ds(start, BLK)],
                    held.at[i, :, half * BLK : (half + 1) * BLK],
                    in_sem.at[2 * i + half],
                )
            )
        stores.append(pltpu.make_async_copy(held.at[i], out, out_sem.at[i]))
    farthest_first = [*range(1, count), 0]
    for i in farthest_first:
        loads[2 * i].start()
        loads[2 * i + 1].start()
    for i in farthest_first:
        loads[2 * i].wait()
        loads[2 * i + 1].wait()
        stores[i].start()
    for i in farthest_first:
        stores[i].wait()


def pack(order, x, count):
    rows = x.shape[0]
    piece = jax.ShapeDtypeStruct((rows, 2 * BLK), jnp.float32)
    hbm = pl.BlockSpec(memory_space=pltpu.HBM)
    return pl.pallas_call(
        pack_kernel,
        out_shape=[piece] * count,
        in_specs=[pl.BlockSpec(memory_space=pltpu.SMEM), hbm],
        out_specs=[hbm] * count,
        scratch_shapes=[
            pltpu.VMEM((count, rows, 2 * BLK), jnp.float32),
            pltpu.SemaphoreType.DMA((2 * count,)),
            pltpu.SemaphoreType.DMA((count,)),
        ],
        name="pack",
    )(order, x)


def unpack_kernel(place_ref, *refs):
    pieces, out_ref, held, in_sem, out_sem = refs[:-4], *refs[-4:]
    width = 2 * BLK
    loads, stores = [], []
    for i, piece in enumerate(pieces):
        start = pl.multiple_of(place_ref[i] * width, width)
        loads.append(pltpu.make_async_copy(piece, held.at[i], in_sem.at[i]))
        stores.append(
            pltpu.make_async_copy(held.at[i], out_ref.at[:, pl.ds(start, width)], out_sem.at[i])
        )
    for load in loads:
        load.start()
    for load, store in zip(loads, stores):
        load.wait()
        store.start()
    for store in stores:
        store.wait()


def unpack(place, pieces):
    rows, width = pieces[0].shape
    count = len(pieces)
    hbm = pl.BlockSpec(memory_space=pltpu.HBM)
    return pl.pallas_call(
        unpack_kernel,
        out_shape=jax.ShapeDtypeStruct((rows, count * width), jnp.float32),
        in_specs=[pl.BlockSpec(memory_space=pltpu.SMEM)] + [hbm] * count,
        out_specs=hbm,
        scratch_shapes=[
            pltpu.VMEM((count, rows, width), jnp.float32),
            pltpu.SemaphoreType.DMA((count,)),
            pltpu.SemaphoreType.DMA((count,)),
        ],
        name="unpack",
    )(place, *pieces)


def first_kernel(count, given, source_ref, *refs):
    pieces = refs[:count]
    refs = refs[count:]
    terms, refs = refs[: 3 * given], refs[3 * given :]
    new_upper_ref, new_lower_ref, upper_ref, lower_ref, aug_ref, sem = refs
    rows = pieces[0].shape[0]
    copies = []
    for i, piece in enumerate(pieces):
        start = pl.multiple_of(source_ref[i] * rows, rows)
        for half, target in enumerate((upper_ref, lower_ref)):
            copies.append(
                pltpu.make_async_copy(
                    piece.at[:, half * BLK : (half + 1) * BLK],
                    target.at[pl.ds(start, rows), :],
                    sem.at[2 * i + half],
                )
            )
    for copy in copies:
        copy.start()
    for copy in copies:
        copy.wait()
    if given:
        cross, upper_sq, lower_sq = (term[...] for term in terms)
    else:
        cross, upper_sq, lower_sq = terms_of(upper_ref[...], lower_ref[...])
    new_upper, new_lower = rotate_pair(upper_ref, lower_ref, cross, upper_sq, lower_sq, aug_ref)
    new_upper_ref[...] = new_upper
    new_lower_ref[...] = new_lower


def first_round(source, pieces, terms):
    rows = pieces[0].shape[0]
    count = len(pieces)
    tokens = rows * count
    block = jax.ShapeDtypeStruct((tokens, BLK), jnp.float32)
    vmem = pl.BlockSpec(memory_space=pltpu.VMEM)
    return pl.pallas_call(
        functools.partial(first_kernel, count, int(bool(terms))),
        out_shape=[block, block],
        in_specs=[pl.BlockSpec(memory_space=pltpu.SMEM)]
        + [pl.BlockSpec(memory_space=pltpu.HBM)] * count
        + [vmem] * len(terms),
        out_specs=[vmem, vmem],
        scratch_shapes=[
            pltpu.VMEM((tokens, BLK), jnp.float32),
            pltpu.VMEM((tokens, BLK), jnp.float32),
            pltpu.VMEM((2, BLK, 2 * BLK), jnp.float32),
            pltpu.SemaphoreType.DMA((2 * count,)),
        ],
        compiler_params=pltpu.CompilerParams(vmem_limit_bytes=VMEM_LIMIT),
        name="first_round",
    )(source, *pieces, *terms)


def last_kernel(count, given, source_ref, upper_ref, lower_ref, *refs):
    terms, refs = refs[: 3 * given], refs[3 * given :]
    outs = refs[:count]
    result_ref, aug_ref, sem = refs[count:]
    rows = outs[0].shape[0]
    if given:
        cross, upper_sq, lower_sq = (term[...] for term in terms)
    else:
        cross, upper_sq, lower_sq = terms_of(upper_ref[...], lower_ref[...])
    new_upper, new_lower = rotate_pair(upper_ref, lower_ref, cross, upper_sq, lower_sq, aug_ref)
    result_ref[:, :BLK] = new_upper
    result_ref[:, BLK:] = new_lower
    copies = []
    for i, out in enumerate(outs):
        start = pl.multiple_of(source_ref[i] * rows, rows)
        copies.append(pltpu.make_async_copy(result_ref.at[pl.ds(start, rows), :], out, sem.at[i]))
    for copy in copies:
        copy.start()
    for copy in copies:
        copy.wait()


def last_round(source, upper, lower, terms):
    tokens = upper.shape[0]
    count = source.shape[0]
    piece = jax.ShapeDtypeStruct((tokens // count, 2 * BLK), jnp.float32)
    vmem = pl.BlockSpec(memory_space=pltpu.VMEM)
    return pl.pallas_call(
        functools.partial(last_kernel, count, int(bool(terms))),
        out_shape=[piece] * count,
        in_specs=[pl.BlockSpec(memory_space=pltpu.SMEM), vmem, vmem] + [vmem] * len(terms),
        out_specs=[pl.BlockSpec(memory_space=pltpu.HBM)] * count,
        scratch_shapes=[
            pltpu.VMEM((tokens, 2 * BLK), jnp.float32),
            pltpu.VMEM((2, BLK, 2 * BLK), jnp.float32),
            pltpu.SemaphoreType.DMA((count,)),
        ],
        compiler_params=pltpu.CompilerParams(vmem_limit_bytes=VMEM_LIMIT),
        name="last_round",
    )(source, upper, lower, *terms)


def on_device(activations, plan):
    token_axes = ("rows", "sub")
    all_axes = ("rows", "cols", "sub")
    subs = lax.axis_size("sub")
    columns = lax.axis_size("cols")
    column = lax.axis_index("cols")
    block_count = activations.shape[1] // BLK
    pairs = block_count // 2
    token_group = lax.axis_size(token_axes)
    token_index = lax.axis_index(token_axes)
    teams = token_group // pairs
    assert teams * pairs == token_group and pairs & (pairs - 1) == 0
    member = token_index % pairs
    shifts = [0] + list(range(pairs - 1, 0, -1))
    partner = jnp.bitwise_xor(member, jnp.array(shifts, dtype=jnp.int32))
    backwards = column % 2 == 1

    def pair_of(member):
        return jnp.where(backwards, pairs - 1 - member, member)

    def exchange(pieces):
        arrived = [pieces[0]]
        for shift, piece in zip(shifts[1:], pieces[1:]):
            route = [(t, t ^ shift) for t in range(token_group)]
            arrived.append(lax.ppermute(piece, token_axes, route))
        return arrived

    def added_up(upper, lower):
        groups = [[team * pairs + m for team in range(teams)] for m in range(pairs)]
        total = []
        for term in terms_of(upper, lower):
            full = term
            for step in range(1, teams):
                route = [
                    (group[i], group[(i + step) % teams]) for group in groups for i in range(teams)
                ]
                full = full + lax.ppermute(term, token_axes, route)
            total.append(full)
        return total

    local_order = (
        lax.dynamic_slice_in_dim(plan[0], column * block_count, block_count) - column * block_count
    )
    order = jnp.take(local_order.reshape(pairs, 2), pair_of(partner), axis=0).reshape(-1)
    pieces = exchange(pack(order, activations, pairs))

    terms = []
    if teams > 1:
        canonical = jnp.concatenate(pieces, axis=0)
        terms = added_up(canonical[:, :BLK], canonical[:, BLK:])
    upper, lower = first_round(partner, pieces, terms)

    def device_of(pair):
        home, inner = divmod(pair, pairs)
        return home, pairs - 1 - inner if home % 2 else inner

    total_pairs = columns * pairs
    chain = column * pairs + pair_of(member)
    first = chain == 0
    final = chain == total_pairs - 1

    def along(block, distance):
        route = []
        for pair in range(total_pairs):
            if 0 <= pair + distance < total_pairs:
                for team in range(teams):
                    ends = []
                    for one in (pair, pair + distance):
                        home, inner = device_of(one)
                        row, sub = divmod(team * pairs + inner, subs)
                        ends.append((row * columns + home) * subs + sub)
                    route.append(tuple(ends))
        return lax.ppermute(block, all_axes, route)

    arriving = along(jnp.where(first, lower, upper), 1)
    leaving = along(lower, -1)
    next_upper = jnp.where(first, upper, arriving)
    next_lower = jnp.where(final, upper, leaving)

    terms = added_up(next_upper, next_lower) if teams > 1 else []
    pieces = exchange(last_round(partner, next_upper, next_lower, terms))
    return unpack(pair_of(partner), pieces)


def solution(mesh):
    in_specs = (P(("groups", "rows", "sub"), "cols"), P())
    out_specs = P(("groups", "rows", "sub"), "cols")
    return jax.shard_map(
        on_device, mesh=mesh, in_specs=in_specs, out_specs=out_specs, check_vma=False
    )
```

```python
import functools

import jax
import jax.numpy as jnp
from jax import lax
from jax.experimental import pallas as pl
from jax.experimental.pallas import tpu as pltpu
from jax.sharding import PartitionSpec as P

BLK = 256
ROUNDS = 2
PANEL = 64
SUBLANES = 8

epsilon = 1e-06
HIGH = lax.Precision.HIGHEST
VMEM_LIMIT = 40 * 1024 * 1024


def contract(a, b, a_dim, b_dim):
    return lax.dot_general(
        a, b, (((a_dim,), (b_dim,)), ((), ())), precision=HIGH, preferred_element_type=jnp.float32
    )


def iota2(shape, dim):
    return lax.broadcasted_iota(jnp.int32, shape, dim)


def reciprocal(x):
    guess = pl.reciprocal(x, approx=True)
    return guess * (2.0 - x * guess)


def eliminate(blocks):
    width = 2 * PANEL
    shape = (SUBLANES, width)
    tiles = PANEL // SUBLANES
    lines = range(SUBLANES)
    ident = jnp.where(iota2((PANEL, PANEL), 0) == iota2((PANEL, PANEL), 1), 1.0, 0.0).astype(jnp.float32)
    sub = iota2(shape, 0)
    parts, outs = [], []
    for block in blocks:
        whole = jnp.concatenate([block, ident], axis=1)
        parts.append([whole[SUBLANES * v : SUBLANES * (v + 1)] for v in range(tiles)])
        outs.append([])
    for q in range(tiles):
        states = []
        for part in parts:
            columns = [
                [
                    jnp.broadcast_to(part[v][:, SUBLANES * q + j : SUBLANES * q + j + 1], shape)
                    for j in lines
                ]
                for v in range(q, tiles)
            ]
            entry = [
                [jnp.broadcast_to(columns[0][j][i : i + 1, :], shape) for j in range(i + 1)]
                for i in lines
            ]
            rows = [jnp.broadcast_to(part[q][i : i + 1, :], shape) for i in lines]
            states.append((columns, entry, rows, []))
        for s in lines:
            for columns, entry, rows, inverses in states:
                inverse = reciprocal(entry[s][s])
                inverses.append(inverse)
                factors = {i: entry[i][s] * inverse for i in range(s + 1, SUBLANES)}
                for i in range(s + 1, SUBLANES):
                    for j in range(s + 1, i + 1):
                        entry[i][j] = entry[i][j] - factors[i] * entry[j][s]
                for i in range(s + 1, SUBLANES):
                    rows[i] = rows[i] - factors[i] * rows[s]
        for v in range(q + 1, tiles):
            for part, (columns, entry, rows, inverses) in zip(parts, states):
                factors = []
                for s in lines:
                    value = columns[v - q][s]
                    for t in range(s):
                        value = value - factors[t] * entry[s][t]
                    factors.append(value * inverses[s])
                for s in lines:
                    part[v] = part[v] - factors[s] * rows[s]
        for out, (columns, entry, rows, inverses) in zip(outs, states):
            tile = rows[0] * lax.rsqrt(entry[0][0])
            for i in lines[1:]:
                tile = jnp.where(sub == i, rows[i] * lax.rsqrt(entry[i][i]), tile)
            out.append(tile[:, PANEL:])
    return [jnp.concatenate(out, axis=0) for out in outs]


def inverse_factors(work_ref, inv_ref):
    inv_ref[...] = jnp.zeros_like(inv_ref)
    ident = jnp.where(iota2((PANEL, PANEL), 0) == iota2((PANEL, PANEL), 1), 1.0, 0.0).astype(jnp.float32)
    for p in range(BLK // PANEL):
        top = p * PANEL
        end = top + PANEL
        invs = eliminate([work_ref[m, top:end, top:end] for m in range(2)])
        for m in range(2):
            work_ref[m, top:end, top:end] = ident
            rows = contract(invs[m], work_ref[m, top:end, :], 1, 0)
            inv_ref[m, top:end, :end] = rows[:, :end]
            if end < BLK:
                work_ref[m, end:, top:end] = jnp.zeros((BLK - end, PANEL), jnp.float32)
                work_ref[m, end:, :] = work_ref[m, end:, :] - contract(rows[:, end:], rows, 0, 0)


def rotate_pair(upper_ref, lower_ref, cross, upper_sq, lower_sq, work_ref, inv_ref):
    square = (BLK, BLK)
    diagonal = iota2(square, 0) == iota2(square, 1)
    ident = jnp.where(diagonal, 1.0, 0.0).astype(jnp.float32)
    upper_sq = jnp.sum(
        jnp.where(diagonal, jnp.broadcast_to(upper_sq, square), 0.0), axis=1, keepdims=True
    )
    corr = cross * lax.rsqrt(upper_sq + epsilon) * lax.rsqrt(lower_sq + epsilon)
    work_ref[0] = ident + contract(corr, corr, 1, 1)
    work_ref[1] = ident + contract(corr, corr, 0, 0)
    inverse_factors(work_ref, inv_ref)
    upper = upper_ref[...]
    lower = lower_ref[...]
    mixed_upper = upper + contract(lower, corr, 1, 1)
    mixed_lower = lower - contract(upper, corr, 1, 0)
    new_upper = contract(mixed_upper, inv_ref[0], 1, 1)
    new_lower = contract(mixed_lower, inv_ref[1], 1, 1)
    return new_upper, new_lower


def terms_of(upper, lower):
    return (
        contract(upper, lower, 0, 0),
        jnp.sum(upper * upper, axis=0, keepdims=True),
        jnp.sum(lower * lower, axis=0, keepdims=True),
    )


def pack_kernel(order_ref, x_ref, *refs):
    outs, held, in_sem, out_sem = refs[:-3], *refs[-3:]
    count = len(outs)
    loads, stores = [], []
    for i, out in enumerate(outs):
        for half in range(2):
            start = pl.multiple_of(order_ref[2 * i + half] * BLK, BLK)
            loads.append(
                pltpu.make_async_copy(
                    x_ref.at[:, pl.ds(start, BLK)],
                    held.at[i, :, half * BLK : (half + 1) * BLK],
                    in_sem.at[2 * i + half],
                )
            )
        stores.append(pltpu.make_async_copy(held.at[i], out, out_sem.at[i]))
    farthest_first = [*range(1, count), 0]
    for i in farthest_first:
        loads[2 * i].start()
        loads[2 * i + 1].start()
    for i in farthest_first:
        loads[2 * i].wait()
        loads[2 * i + 1].wait()
        stores[i].start()
    for i in farthest_first:
        stores[i].wait()


def pack(order, x, count):
    rows = x.shape[0]
    piece = jax.ShapeDtypeStruct((rows, 2 * BLK), jnp.float32)
    hbm = pl.BlockSpec(memory_space=pltpu.HBM)
    return pl.pallas_call(
        pack_kernel,
        out_shape=[piece] * count,
        in_specs=[pl.BlockSpec(memory_space=pltpu.SMEM), hbm],
        out_specs=[hbm] * count,
        scratch_shapes=[
            pltpu.VMEM((count, rows, 2 * BLK), jnp.float32),
            pltpu.SemaphoreType.DMA((2 * count,)),
            pltpu.SemaphoreType.DMA((count,)),
        ],
        name="pack",
    )(order, x)


def unpack_kernel(place_ref, *refs):
    pieces, out_ref, held, in_sem, out_sem = refs[:-4], *refs[-4:]
    width = 2 * BLK
    loads, stores = [], []
    for i, piece in enumerate(pieces):
        start = pl.multiple_of(place_ref[i] * width, width)
        loads.append(pltpu.make_async_copy(piece, held.at[i], in_sem.at[i]))
        stores.append(
            pltpu.make_async_copy(held.at[i], out_ref.at[:, pl.ds(start, width)], out_sem.at[i])
        )
    for load in loads:
        load.start()
    for load, store in zip(loads, stores):
        load.wait()
        store.start()
    for store in stores:
        store.wait()


def unpack(place, pieces):
    rows, width = pieces[0].shape
    count = len(pieces)
    hbm = pl.BlockSpec(memory_space=pltpu.HBM)
    return pl.pallas_call(
        unpack_kernel,
        out_shape=jax.ShapeDtypeStruct((rows, count * width), jnp.float32),
        in_specs=[pl.BlockSpec(memory_space=pltpu.SMEM)] + [hbm] * count,
        out_specs=hbm,
        scratch_shapes=[
            pltpu.VMEM((count, rows, width), jnp.float32),
            pltpu.SemaphoreType.DMA((count,)),
            pltpu.SemaphoreType.DMA((count,)),
        ],
        name="unpack",
    )(place, *pieces)


def first_kernel(count, given, source_ref, *refs):
    pieces = refs[:count]
    refs = refs[count:]
    terms, refs = refs[: 3 * given], refs[3 * given :]
    new_upper_ref, new_lower_ref, upper_ref, lower_ref, work_ref, inv_ref, sem = refs
    rows = pieces[0].shape[0]
    copies = []
    for i, piece in enumerate(pieces):
        start = pl.multiple_of(source_ref[i] * rows, rows)
        for half, target in enumerate((upper_ref, lower_ref)):
            copies.append(
                pltpu.make_async_copy(
                    piece.at[:, half * BLK : (half + 1) * BLK],
                    target.at[pl.ds(start, rows), :],
                    sem.at[2 * i + half],
                )
            )
    for copy in copies:
        copy.start()
    for copy in copies:
        copy.wait()
    if given:
        cross, upper_sq, lower_sq = (term[...] for term in terms)
    else:
        cross, upper_sq, lower_sq = terms_of(upper_ref[...], lower_ref[...])
    new_upper, new_lower = rotate_pair(
        upper_ref, lower_ref, cross, upper_sq, lower_sq, work_ref, inv_ref
    )
    new_upper_ref[...] = new_upper
    new_lower_ref[...] = new_lower


def first_round(source, pieces, terms):
    rows = pieces[0].shape[0]
    count = len(pieces)
    tokens = rows * count
    block = jax.ShapeDtypeStruct((tokens, BLK), jnp.float32)
    vmem = pl.BlockSpec(memory_space=pltpu.VMEM)
    return pl.pallas_call(
        functools.partial(first_kernel, count, int(bool(terms))),
        out_shape=[block, block],
        in_specs=[pl.BlockSpec(memory_space=pltpu.SMEM)]
        + [pl.BlockSpec(memory_space=pltpu.HBM)] * count
        + [vmem] * len(terms),
        out_specs=[vmem, vmem],
        scratch_shapes=[
            pltpu.VMEM((tokens, BLK), jnp.float32),
            pltpu.VMEM((tokens, BLK), jnp.float32),
            pltpu.VMEM((2, BLK, BLK), jnp.float32),
            pltpu.VMEM((2, BLK, BLK), jnp.float32),
            pltpu.SemaphoreType.DMA((2 * count,)),
        ],
        compiler_params=pltpu.CompilerParams(vmem_limit_bytes=VMEM_LIMIT),
        name="first_round",
    )(source, *pieces, *terms)


def last_kernel(count, given, source_ref, upper_ref, lower_ref, *refs):
    terms, refs = refs[: 3 * given], refs[3 * given :]
    outs = refs[:count]
    result_ref, work_ref, inv_ref, sem = refs[count:]
    rows = outs[0].shape[0]
    if given:
        cross, upper_sq, lower_sq = (term[...] for term in terms)
    else:
        cross, upper_sq, lower_sq = terms_of(upper_ref[...], lower_ref[...])
    new_upper, new_lower = rotate_pair(
        upper_ref, lower_ref, cross, upper_sq, lower_sq, work_ref, inv_ref
    )
    result_ref[:, :BLK] = new_upper
    result_ref[:, BLK:] = new_lower
    copies = []
    for i, out in enumerate(outs):
        start = pl.multiple_of(source_ref[i] * rows, rows)
        copies.append(pltpu.make_async_copy(result_ref.at[pl.ds(start, rows), :], out, sem.at[i]))
    for copy in copies:
        copy.start()
    for copy in copies:
        copy.wait()


def last_round(source, upper, lower, terms):
    tokens = upper.shape[0]
    count = source.shape[0]
    piece = jax.ShapeDtypeStruct((tokens // count, 2 * BLK), jnp.float32)
    vmem = pl.BlockSpec(memory_space=pltpu.VMEM)
    return pl.pallas_call(
        functools.partial(last_kernel, count, int(bool(terms))),
        out_shape=[piece] * count,
        in_specs=[pl.BlockSpec(memory_space=pltpu.SMEM), vmem, vmem] + [vmem] * len(terms),
        out_specs=[pl.BlockSpec(memory_space=pltpu.HBM)] * count,
        scratch_shapes=[
            pltpu.VMEM((tokens, 2 * BLK), jnp.float32),
            pltpu.VMEM((2, BLK, BLK), jnp.float32),
            pltpu.VMEM((2, BLK, BLK), jnp.float32),
            pltpu.SemaphoreType.DMA((count,)),
        ],
        compiler_params=pltpu.CompilerParams(vmem_limit_bytes=VMEM_LIMIT),
        name="last_round",
    )(source, upper, lower, *terms)


def on_device(activations, plan):
    token_axes = ("rows", "sub")
    all_axes = ("rows", "cols", "sub")
    subs = lax.axis_size("sub")
    columns = lax.axis_size("cols")
    column = lax.axis_index("cols")
    block_count = activations.shape[1] // BLK
    pairs = block_count // 2
    token_group = lax.axis_size(token_axes)
    token_index = lax.axis_index(token_axes)
    teams = token_group // pairs
    assert teams * pairs == token_group and pairs & (pairs - 1) == 0
    member = token_index % pairs
    shifts = [0] + list(range(pairs - 1, 0, -1))
    partner = jnp.bitwise_xor(member, jnp.array(shifts, dtype=jnp.int32))
    backwards = column % 2 == 1

    def pair_of(member):
        return jnp.where(backwards, pairs - 1 - member, member)

    def exchange(pieces):
        arrived = [pieces[0]]
        for shift, piece in zip(shifts[1:], pieces[1:]):
            route = [(t, t ^ shift) for t in range(token_group)]
            arrived.append(lax.ppermute(piece, token_axes, route))
        return arrived

    def added_up(upper, lower):
        groups = [[team * pairs + m for team in range(teams)] for m in range(pairs)]
        total = []
        for term in terms_of(upper, lower):
            full = term
            for step in range(1, teams):
                route = [
                    (group[i], group[(i + step) % teams]) for group in groups for i in range(teams)
                ]
                full = full + lax.ppermute(term, token_axes, route)
            total.append(full)
        return total

    local_order = (
        lax.dynamic_slice_in_dim(plan[0], column * block_count, block_count) - column * block_count
    )
    order = jnp.take(local_order.reshape(pairs, 2), pair_of(partner), axis=0).reshape(-1)
    pieces = exchange(pack(order, activations, pairs))

    terms = []
    if teams > 1:
        canonical = jnp.concatenate(pieces, axis=0)
        terms = added_up(canonical[:, :BLK], canonical[:, BLK:])
    upper, lower = first_round(partner, pieces, terms)

    def device_of(pair):
        home, inner = divmod(pair, pairs)
        return home, pairs - 1 - inner if home % 2 else inner

    total_pairs = columns * pairs
    chain = column * pairs + pair_of(member)
    first = chain == 0
    final = chain == total_pairs - 1

    def along(block, distance):
        route = []
        for pair in range(total_pairs):
            if 0 <= pair + distance < total_pairs:
                for team in range(teams):
                    ends = []
                    for one in (pair, pair + distance):
                        home, inner = device_of(one)
                        row, sub = divmod(team * pairs + inner, subs)
                        ends.append((row * columns + home) * subs + sub)
                    route.append(tuple(ends))
        return lax.ppermute(block, all_axes, route)

    arriving = along(jnp.where(first, lower, upper), 1)
    leaving = along(lower, -1)
    next_upper = jnp.where(first, upper, arriving)
    next_lower = jnp.where(final, upper, leaving)

    terms = added_up(next_upper, next_lower) if teams > 1 else []
    pieces = exchange(last_round(partner, next_upper, next_lower, terms))
    return unpack(pair_of(partner), pieces)


def solution(mesh):
    in_specs = (P(("groups", "rows", "sub"), "cols"), P())
    out_specs = P(("groups", "rows", "sub"), "cols")
    return jax.shard_map(
        on_device, mesh=mesh, in_specs=in_specs, out_specs=out_specs, check_vma=False
    )
```

```python
import functools

import jax
import jax.numpy as jnp
from jax import lax
from jax.experimental import pallas as pl
from jax.experimental.pallas import tpu as pltpu
from jax.sharding import PartitionSpec as P

BLK = 256
ROUNDS = 2
PANEL = 64
SUBLANES = 8

epsilon = 1e-06
HIGH = lax.Precision.HIGHEST
VMEM_LIMIT = 16 * 1024 * 1024
TEAM_CHIPS = 2
SQUARES = 8


def contract(a, b, a_dim, b_dim):
    return lax.dot_general(
        a, b, (((a_dim,), (b_dim,)), ((), ())), precision=HIGH, preferred_element_type=jnp.float32
    )


def iota2(shape, dim):
    return lax.broadcasted_iota(jnp.int32, shape, dim)


def reciprocal(x):
    guess = pl.reciprocal(x, approx=True)
    return guess * (2.0 - x * guess)


def eliminate(blocks):
    width = 2 * PANEL
    shape = (SUBLANES, width)
    tiles = PANEL // SUBLANES
    lines = range(SUBLANES)
    ident = jnp.where(iota2((PANEL, PANEL), 0) == iota2((PANEL, PANEL), 1), 1.0, 0.0).astype(jnp.float32)
    sub = iota2(shape, 0)
    parts, outs = [], []
    for block in blocks:
        whole = jnp.concatenate([block, ident], axis=1)
        parts.append([whole[SUBLANES * v : SUBLANES * (v + 1)] for v in range(tiles)])
        outs.append([])
    for q in range(tiles):
        states = []
        for part in parts:
            columns = [
                [
                    jnp.broadcast_to(part[v][:, SUBLANES * q + j : SUBLANES * q + j + 1], shape)
                    for j in lines
                ]
                for v in range(q, tiles)
            ]
            entry = [
                [jnp.broadcast_to(columns[0][j][i : i + 1, :], shape) for j in range(i + 1)]
                for i in lines
            ]
            rows = [jnp.broadcast_to(part[q][i : i + 1, :], shape) for i in lines]
            states.append((columns, entry, rows, []))
        for s in lines:
            for columns, entry, rows, inverses in states:
                inverse = reciprocal(entry[s][s])
                inverses.append(inverse)
                factors = {i: entry[i][s] * inverse for i in range(s + 1, SUBLANES)}
                for i in range(s + 1, SUBLANES):
                    for j in range(s + 1, i + 1):
                        entry[i][j] = entry[i][j] - factors[i] * entry[j][s]
                for i in range(s + 1, SUBLANES):
                    rows[i] = rows[i] - factors[i] * rows[s]
        for v in range(q + 1, tiles):
            for part, (columns, entry, rows, inverses) in zip(parts, states):
                factors = []
                for s in lines:
                    value = columns[v - q][s]
                    for t in range(s):
                        value = value - factors[t] * entry[s][t]
                    factors.append(value * inverses[s])
                for s in lines:
                    part[v] = part[v] - factors[s] * rows[s]
        for out, (columns, entry, rows, inverses) in zip(outs, states):
            tile = rows[0] * lax.rsqrt(entry[0][0])
            for i in lines[1:]:
                tile = jnp.where(sub == i, rows[i] * lax.rsqrt(entry[i][i]), tile)
            out.append(tile[:, PANEL:])
    return [jnp.concatenate(out, axis=0) for out in outs]


def inverse_factors(work_ref, inv_ref):
    inv_ref[...] = jnp.zeros_like(inv_ref)
    ident = jnp.where(iota2((PANEL, PANEL), 0) == iota2((PANEL, PANEL), 1), 1.0, 0.0).astype(jnp.float32)
    for p in range(BLK // PANEL):
        top = p * PANEL
        end = top + PANEL
        invs = eliminate([work_ref[m, top:end, top:end] for m in range(2)])
        for m in range(2):
            work_ref[m, top:end, top:end] = ident
            rows = contract(invs[m], work_ref[m, top:end, :], 1, 0)
            inv_ref[m, top:end, :end] = rows[:, :end]
            if end < BLK:
                work_ref[m, end:, top:end] = jnp.zeros((BLK - end, PANEL), jnp.float32)
                work_ref[m, end:, :] = work_ref[m, end:, :] - contract(rows[:, end:], rows, 0, 0)


def pair_terms(upper, lower):
    upper_sq = jnp.sum(upper * upper, axis=0, keepdims=True)
    lower_sq = jnp.sum(lower * lower, axis=0, keepdims=True)
    line = iota2((SQUARES, BLK), 0)
    squares = jnp.where(line == 0, upper_sq, jnp.where(line == 1, lower_sq, 0.0))
    return contract(upper, lower, 0, 0), squares


def rotated(upper_ref, lower_ref, terms, work_ref, inv_ref):
    square = (BLK, BLK)
    diagonal = iota2(square, 0) == iota2(square, 1)
    ident = jnp.where(diagonal, 1.0, 0.0).astype(jnp.float32)
    upper_sq, lower_sq = terms[BLK : BLK + 1], terms[BLK + 1 : BLK + 2]
    upper_sq = jnp.sum(
        jnp.where(diagonal, jnp.broadcast_to(upper_sq, square), 0.0), axis=1, keepdims=True
    )
    corr = terms[:BLK] * lax.rsqrt(upper_sq + epsilon) * lax.rsqrt(lower_sq + epsilon)
    work_ref[0] = ident + contract(corr, corr, 1, 1)
    work_ref[1] = ident + contract(corr, corr, 0, 0)
    inverse_factors(work_ref, inv_ref)
    upper = upper_ref[...]
    lower = lower_ref[...]
    mixed_upper = upper + contract(lower, corr, 1, 1)
    mixed_lower = lower - contract(upper, corr, 1, 0)
    new_upper = contract(mixed_upper, inv_ref[0], 1, 1)
    new_lower = contract(mixed_lower, inv_ref[1], 1, 1)
    return new_upper, new_lower


SMEM_SPEC = pl.BlockSpec(memory_space=pltpu.SMEM)
VMEM_SPEC = pl.BlockSpec(memory_space=pltpu.VMEM)
HBM_SPEC = pl.BlockSpec(memory_space=pltpu.HBM)


def call(kernel, name, out_shape, in_specs, out_specs, scratch, micros):
    return pl.pallas_call(
        kernel,
        out_shape=out_shape,
        in_specs=in_specs,
        out_specs=out_specs,
        scratch_shapes=scratch,
        compiler_params=pltpu.CompilerParams(vmem_limit_bytes=VMEM_LIMIT),
        cost_estimate=pl.CostEstimate(
            flops=int(micros * 1e9), bytes_accessed=1 << 20, transcendentals=0
        ),
        name=name,
    )


def f32(*shape):
    return jax.ShapeDtypeStruct(shape, jnp.float32)


def pack_kernel(order_ref, x_ref, *refs):
    outs, held, in_sem, out_sem = refs[:-3], *refs[-3:]
    loads, stores = [], []
    for i, out in enumerate(outs):
        for half in range(2):
            start = pl.multiple_of(order_ref[2 * i + half] * BLK, BLK)
            loads.append(
                pltpu.make_async_copy(
                    x_ref.at[:, pl.ds(start, BLK)],
                    held.at[i, :, half * BLK : (half + 1) * BLK],
                    in_sem.at[2 * i + half],
                )
            )
        stores.append(pltpu.make_async_copy(held.at[i], out, out_sem.at[i]))
    for load in loads:
        load.start()
    for i, store in enumerate(stores):
        loads[2 * i].wait()
        loads[2 * i + 1].wait()
        store.start()
    for store in stores:
        store.wait()


def pack(order, x, count):
    rows = x.shape[0]
    return call(
        pack_kernel,
        "pack",
        [f32(rows, 2 * BLK)] * count,
        [SMEM_SPEC, HBM_SPEC],
        [HBM_SPEC] * count,
        [
            pltpu.VMEM((count, rows, 2 * BLK), jnp.float32),
            pltpu.SemaphoreType.DMA((2 * count,)),
            pltpu.SemaphoreType.DMA((count,)),
        ],
        3,
    )(order, x)


def unpack_kernel(place_ref, *refs):
    pieces, out_ref, held, in_sem, out_sem = refs[:-4], *refs[-4:]
    width = 2 * BLK
    loads, stores = [], []
    for i, piece in enumerate(pieces):
        start = pl.multiple_of(place_ref[i] * width, width)
        loads.append(pltpu.make_async_copy(piece, held.at[i], in_sem.at[i]))
        stores.append(
            pltpu.make_async_copy(held.at[i], out_ref.at[:, pl.ds(start, width)], out_sem.at[i])
        )
    for load in loads:
        load.start()
    for load, store in zip(loads, stores):
        load.wait()
        store.start()
    for store in stores:
        store.wait()


def unpack(place, pieces):
    rows, width = pieces[0].shape
    count = len(pieces)
    return call(
        unpack_kernel,
        "unpack",
        f32(rows, count * width),
        [SMEM_SPEC] + [HBM_SPEC] * count,
        HBM_SPEC,
        [
            pltpu.VMEM((count, rows, width), jnp.float32),
            pltpu.SemaphoreType.DMA((count,)),
            pltpu.SemaphoreType.DMA((count,)),
        ],
        3,
    )(place, *pieces)


def gather_terms_kernel(source_ref, *refs):
    pieces, (upper_ref, lower_ref, terms_ref) = refs[:-3], refs[-3:]
    rows = pieces[0].shape[0]
    for i, piece in enumerate(pieces):
        start = pl.multiple_of(source_ref[i] * rows, rows)
        upper_ref[pl.ds(start, rows), :] = piece[:, :BLK]
        lower_ref[pl.ds(start, rows), :] = piece[:, BLK:]
    terms_ref[:BLK], terms_ref[BLK:] = pair_terms(upper_ref[...], lower_ref[...])


def gather_terms(source, pieces):
    tokens = pieces[0].shape[0] * len(pieces)
    return call(
        gather_terms_kernel,
        "gather_terms",
        [f32(tokens, BLK), f32(tokens, BLK), f32(BLK + SQUARES, BLK)],
        [SMEM_SPEC] + [VMEM_SPEC] * len(pieces),
        [VMEM_SPEC] * 3,
        [],
        2,
    )(source, *pieces)


def choose_terms_kernel(flag_ref, *refs):
    uppers, lowers, (upper_ref, lower_ref, terms_ref) = refs[:2], refs[2:4], refs[4:]
    for at, choices, out_ref in ((0, uppers, upper_ref), (1, lowers, lower_ref)):
        chosen = flag_ref[at] == 1

        @pl.when(chosen)
        def _():
            out_ref[...] = choices[0][...]

        @pl.when(jnp.logical_not(chosen))
        def _():
            out_ref[...] = choices[1][...]

    terms_ref[:BLK], terms_ref[BLK:] = pair_terms(upper_ref[...], lower_ref[...])


def choose_terms(flags, uppers, lowers):
    tokens = uppers[0].shape[0]
    return call(
        choose_terms_kernel,
        "choose_terms",
        [f32(tokens, BLK), f32(tokens, BLK), f32(BLK + SQUARES, BLK)],
        [SMEM_SPEC] + [VMEM_SPEC] * 4,
        [VMEM_SPEC] * 3,
        [],
        2,
    )(flags, *uppers, *lowers)


def total_terms(refs):
    total = refs[0][...]
    for ref in refs[1:]:
        total = total + ref[...]
    return total


def rotate_kernel(upper_ref, lower_ref, *refs):
    terms, (new_upper_ref, new_lower_ref, work_ref, inv_ref) = refs[:-4], refs[-4:]
    new_upper_ref[...], new_lower_ref[...] = rotated(
        upper_ref, lower_ref, total_terms(terms), work_ref, inv_ref
    )


def factor_scratch():
    return [pltpu.VMEM((2, BLK, BLK), jnp.float32), pltpu.VMEM((2, BLK, BLK), jnp.float32)]


def rotate(upper, lower, terms):
    tokens = upper.shape[0]
    return call(
        rotate_kernel,
        "rotate",
        [f32(tokens, BLK), f32(tokens, BLK)],
        [VMEM_SPEC] * (2 + len(terms)),
        [VMEM_SPEC] * 2,
        factor_scratch(),
        15,
    )(upper, lower, *terms)


def rotate_out_kernel(count, source_ref, upper_ref, lower_ref, *refs):
    terms, refs = refs[: -3 - count], refs[-3 - count :]
    outs, (result_ref, work_ref, inv_ref) = refs[:count], refs[count:]
    result_ref[:, :BLK], result_ref[:, BLK:] = rotated(
        upper_ref, lower_ref, total_terms(terms), work_ref, inv_ref
    )
    rows = outs[0].shape[0]
    for i, out in enumerate(outs):
        start = pl.multiple_of(source_ref[i] * rows, rows)
        out[...] = result_ref[pl.ds(start, rows), :]


def rotate_out(source, upper, lower, terms):
    tokens = upper.shape[0]
    count = source.shape[0]
    return call(
        functools.partial(rotate_out_kernel, count),
        "rotate_out",
        [f32(tokens // count, 2 * BLK)] * count,
        [SMEM_SPEC] + [VMEM_SPEC] * (2 + len(terms)),
        [VMEM_SPEC] * count,
        [pltpu.VMEM((tokens, 2 * BLK), jnp.float32)] + factor_scratch(),
        15,
    )(source, upper, lower, *terms)


def on_device(activations, plan):
    token_axes = ("rows", "sub")
    all_axes = ("rows", "cols", "sub")
    subs = lax.axis_size("sub")
    columns = lax.axis_size("cols")
    column = lax.axis_index("cols")
    block_count = activations.shape[1] // BLK
    pairs = block_count // 2
    token_group = lax.axis_size(token_axes)
    team = min(pairs, TEAM_CHIPS * subs, token_group)
    teams = token_group // team
    held = pairs // team
    assert team * teams == token_group and team * held == pairs and team & (team - 1) == 0
    member = lax.axis_index(token_axes) % team
    shifts = [0] + list(range(team - 1, 0, -1))
    partner = jnp.bitwise_xor(member, jnp.array(shifts, dtype=jnp.int32))
    backwards = column % 2 == 1

    def place_of(member):
        return jnp.where(backwards, team - 1 - member, member)

    def exchange(pieces):
        arrived = [pieces[0]]
        for shift, piece in zip(shifts[1:], pieces[1:]):
            route = [(t, t ^ shift) for t in range(token_group)]
            arrived.append(lax.ppermute(piece, token_axes, route))
        return arrived

    def shared(terms):
        gathered = [terms]
        for step in range(1, teams):
            route = [(t, (t + step * team) % token_group) for t in range(token_group)]
            gathered.append(lax.ppermute(terms, token_axes, route))
        return gathered

    def along(block, distance):
        route = []
        for at in range(columns * team):
            if 0 <= at + distance < columns * team:
                for group in range(teams):
                    ends = []
                    for one in (at, at + distance):
                        home, inner = divmod(one, team)
                        inner = team - 1 - inner if home % 2 else inner
                        row, sub = divmod(group * team + inner, subs)
                        ends.append((row * columns + home) * subs + sub)
                    route.append(tuple(ends))
        return lax.ppermute(block, all_axes, route)

    local_order = (
        lax.dynamic_slice_in_dim(plan[0], column * block_count, block_count) - column * block_count
    )
    wanted = [place_of(partner) * held + g for g in range(held)]
    places = jnp.concatenate(wanted)
    order = jnp.take(local_order.reshape(pairs, 2), places, axis=0).reshape(-1)
    pieces = pack(order, activations, held * team)
    pieces = [pieces[g * team : (g + 1) * team] for g in range(held)]
    arrived = [exchange(piece) for piece in pieces]

    chain = column * team + place_of(member)
    first = (chain == 0).astype(jnp.int32)
    final = (chain == columns * team - 1).astype(jnp.int32)
    always = jnp.int32(1)

    ready = [gather_terms(partner, piece) for piece in arrived]
    summed = [shared(terms) for _, _, terms in ready]
    blocks = [rotate(ready[g][0], ready[g][1], summed[g]) for g in range(held)]

    top_upper, top_lower = blocks[-1]
    if held == 1:
        top_upper = jnp.where(first == 1, top_lower, top_upper)
    leaving = along(blocks[0][1], -1)
    arriving = along(top_upper, 1)

    results = [None] * held
    ready = [None] * held
    for g in reversed(range(held)):
        if g == 0:
            uppers, upper_flag = (blocks[0][0], arriving), first
        elif g == 1:
            uppers, upper_flag = (blocks[0][1], blocks[0][0]), first
        else:
            uppers, upper_flag = (blocks[g - 1][0],) * 2, always
        if g == held - 1:
            lowers, lower_flag = (blocks[g][0], leaving), final
        else:
            lowers, lower_flag = (blocks[g + 1][1],) * 2, always
        ready[g] = choose_terms(jnp.stack([upper_flag, lower_flag]), uppers, lowers)
    for g in reversed(range(held)):
        upper, lower, terms = ready[g]
        results[g] = exchange(rotate_out(partner, upper, lower, shared(terms)))
    return unpack(places, [piece for result in results for piece in result])


def solution(mesh):
    in_specs = (P(("groups", "rows", "sub"), "cols"), P())
    out_specs = P(("groups", "rows", "sub"), "cols")
    return jax.shard_map(
        on_device, mesh=mesh, in_specs=in_specs, out_specs=out_specs, check_vma=False
    )
```

```python
import functools

import jax
import jax.numpy as jnp
from jax import lax
from jax.experimental import pallas as pl
from jax.experimental.pallas import tpu as pltpu
from jax.sharding import PartitionSpec as P

BLK = 256
ROUNDS = 2
PANEL = 64
SUBLANES = 8

epsilon = 1e-06
HIGH = lax.Precision.HIGHEST
VMEM_LIMIT = 16 * 1024 * 1024
TEAM_CHIPS = 2
SQUARES = 8
CHUNK = 256


def contract(a, b, a_dim, b_dim):
    return lax.dot_general(
        a, b, (((a_dim,), (b_dim,)), ((), ())), precision=HIGH, preferred_element_type=jnp.float32
    )


def iota2(shape, dim):
    return lax.broadcasted_iota(jnp.int32, shape, dim)


def reciprocal(x):
    guess = pl.reciprocal(x, approx=True)
    return guess * (2.0 - x * guess)


def eliminate(blocks):
    width = 2 * PANEL
    shape = (SUBLANES, width)
    tiles = PANEL // SUBLANES
    lines = range(SUBLANES)
    ident = jnp.where(iota2((PANEL, PANEL), 0) == iota2((PANEL, PANEL), 1), 1.0, 0.0).astype(jnp.float32)
    sub = iota2(shape, 0)
    parts, outs = [], []
    for block in blocks:
        whole = jnp.concatenate([block, ident], axis=1)
        parts.append([whole[SUBLANES * v : SUBLANES * (v + 1)] for v in range(tiles)])
        outs.append([])
    for q in range(tiles):
        states = []
        for part in parts:
            columns = [
                [
                    jnp.broadcast_to(part[v][:, SUBLANES * q + j : SUBLANES * q + j + 1], shape)
                    for j in lines
                ]
                for v in range(q, tiles)
            ]
            entry = [
                [jnp.broadcast_to(columns[0][j][i : i + 1, :], shape) for j in range(i + 1)]
                for i in lines
            ]
            rows = [jnp.broadcast_to(part[q][i : i + 1, :], shape) for i in lines]
            states.append((columns, entry, rows, []))
        for s in lines:
            for columns, entry, rows, inverses in states:
                inverse = reciprocal(entry[s][s])
                inverses.append(inverse)
                factors = {i: entry[i][s] * inverse for i in range(s + 1, SUBLANES)}
                for i in range(s + 1, SUBLANES):
                    for j in range(s + 1, i + 1):
                        entry[i][j] = entry[i][j] - factors[i] * entry[j][s]
                for i in range(s + 1, SUBLANES):
                    rows[i] = rows[i] - factors[i] * rows[s]
        for v in range(q + 1, tiles):
            for part, (columns, entry, rows, inverses) in zip(parts, states):
                factors = []
                for s in lines:
                    value = columns[v - q][s]
                    for t in range(s):
                        value = value - factors[t] * entry[s][t]
                    factors.append(value * inverses[s])
                for s in lines:
                    part[v] = part[v] - factors[s] * rows[s]
        for out, (columns, entry, rows, inverses) in zip(outs, states):
            tile = rows[0] * lax.rsqrt(entry[0][0])
            for i in lines[1:]:
                tile = jnp.where(sub == i, rows[i] * lax.rsqrt(entry[i][i]), tile)
            out.append(tile[:, PANEL:])
    return [jnp.concatenate(out, axis=0) for out in outs]


def inverse_factors(work_ref):
    lane = iota2((PANEL, BLK), 1)
    ident = jnp.where(iota2((PANEL, BLK), 0) == lane, 1.0, 0.0).astype(jnp.float32)
    own = lane < PANEL
    own_below = iota2((BLK - PANEL, BLK), 1) < PANEL

    def step(p, _):
        invs = eliminate([work_ref[m, :PANEL, :PANEL] for m in range(2)])
        waiting = jnp.logical_and(lane >= PANEL, lane < BLK - PANEL * p)
        for m in range(2):
            rows = contract(invs[m], jnp.where(own, ident, work_ref[m, :PANEL, :]), 1, 0)
            factors = jnp.where(waiting, rows, 0.0)
            below = jnp.where(own_below, 0.0, work_ref[m, PANEL:, :])
            below = below - contract(factors, rows, 0, 0)[PANEL:]
            work_ref[m, : BLK - PANEL, :] = pltpu.roll(below, BLK - PANEL, 1)
            work_ref[m, BLK - PANEL :, :] = pltpu.roll(rows - factors, BLK - PANEL, 1)
        return 0

    lax.fori_loop(0, BLK // PANEL, step, 0)


def pair_terms(upper_ref, lower_ref, terms_ref):
    tokens = upper_ref.shape[0]
    chunk = min(CHUNK, tokens)
    line = iota2((SQUARES, BLK), 0)
    terms_ref[...] = jnp.zeros_like(terms_ref)

    def step(i, _):
        at = pl.ds(pl.multiple_of(i * chunk, chunk), chunk)
        upper, lower = upper_ref[at, :], lower_ref[at, :]
        upper_sq = jnp.sum(upper * upper, axis=0, keepdims=True)
        lower_sq = jnp.sum(lower * lower, axis=0, keepdims=True)
        squares = jnp.where(line == 0, upper_sq, jnp.where(line == 1, lower_sq, 0.0))
        terms_ref[:BLK] += contract(upper, lower, 0, 0)
        terms_ref[BLK:] += squares
        return 0

    lax.fori_loop(0, tokens // chunk, step, 0)


def rotated(upper_ref, lower_ref, terms, work_ref, corr_ref, store):
    square = (BLK, BLK)
    diagonal = iota2(square, 0) == iota2(square, 1)
    ident = jnp.where(diagonal, 1.0, 0.0).astype(jnp.float32)
    upper_sq, lower_sq = terms[BLK : BLK + 1], terms[BLK + 1 : BLK + 2]
    upper_sq = jnp.sum(
        jnp.where(diagonal, jnp.broadcast_to(upper_sq, square), 0.0), axis=1, keepdims=True
    )
    corr = terms[:BLK] * lax.rsqrt(upper_sq + epsilon) * lax.rsqrt(lower_sq + epsilon)
    corr_ref[...] = corr
    work_ref[0] = ident + contract(corr, corr, 1, 1)
    work_ref[1] = ident + contract(corr, corr, 0, 0)
    inverse_factors(work_ref)
    tokens = upper_ref.shape[0]
    chunk = min(CHUNK, tokens)

    def step(i, _):
        at = pl.ds(pl.multiple_of(i * chunk, chunk), chunk)
        upper, lower = upper_ref[at, :], lower_ref[at, :]
        mixed_upper = upper + contract(lower, corr_ref[...], 1, 1)
        mixed_lower = lower - contract(upper, corr_ref[...], 1, 0)
        store(at, contract(mixed_upper, work_ref[0], 1, 1), contract(mixed_lower, work_ref[1], 1, 1))
        return 0

    lax.fori_loop(0, tokens // chunk, step, 0)


SMEM_SPEC = pl.BlockSpec(memory_space=pltpu.SMEM)
VMEM_SPEC = pl.BlockSpec(memory_space=pltpu.VMEM)
HBM_SPEC = pl.BlockSpec(memory_space=pltpu.HBM)


def call(kernel, name, out_shape, in_specs, out_specs, scratch, micros):
    return pl.pallas_call(
        kernel,
        out_shape=out_shape,
        in_specs=in_specs,
        out_specs=out_specs,
        scratch_shapes=scratch,
        compiler_params=pltpu.CompilerParams(vmem_limit_bytes=VMEM_LIMIT),
        cost_estimate=pl.CostEstimate(
            flops=int(micros * 1e9), bytes_accessed=1 << 20, transcendentals=0
        ),
        name=name,
    )


def f32(*shape):
    return jax.ShapeDtypeStruct(shape, jnp.float32)


class Layout:
    def __init__(self, block_count):
        self.block_count = block_count
        self.pairs = block_count // 2
        self.subs = lax.axis_size("sub")
        self.columns = lax.axis_size("cols")
        self.token_group = lax.axis_size("rows") * self.subs
        self.team = min(self.pairs, TEAM_CHIPS * self.subs, self.token_group)
        self.teams = self.token_group // self.team
        self.held = self.pairs // self.team
        assert self.team * self.teams == self.token_group
        assert self.team * self.held == self.pairs and self.team & (self.team - 1) == 0
        self.shifts = [0] + list(range(self.team - 1, 0, -1))

    def member(self):
        return lax.rem(lax.axis_index("rows") * self.subs + lax.axis_index("sub"), self.team)

    def partner(self, i):
        return lax.bitwise_xor(self.member(), jnp.int32(self.shifts[i]))

    def place_of(self, member):
        backwards = lax.rem(lax.axis_index("cols"), 2) == 1
        return jnp.where(backwards, self.team - 1 - member, member)

    def pair_at(self, g, i):
        return self.place_of(self.partner(i)) * self.held + g

    def first(self):
        return jnp.logical_and(lax.axis_index("cols") == 0, self.place_of(self.member()) == 0)

    def final(self):
        return jnp.logical_and(
            lax.axis_index("cols") == self.columns - 1,
            self.place_of(self.member()) == self.team - 1,
        )


def pack_kernel(layout, plan_ref, x_ref, *refs):
    outs, held, in_sem, out_sem = refs[:-3], *refs[-3:]
    base = lax.axis_index("cols") * layout.block_count
    loads, stores = [], []
    for i, out in enumerate(outs):
        pair = layout.pair_at(*divmod(i, layout.team))
        for half in range(2):
            block = plan_ref[0, base + 2 * pair + half] - base
            start = pl.multiple_of(block * BLK, BLK)
            loads.append(
                pltpu.make_async_copy(
                    x_ref.at[:, pl.ds(start, BLK)],
                    held.at[i, :, half * BLK : (half + 1) * BLK],
                    in_sem.at[2 * i + half],
                )
            )
        stores.append(pltpu.make_async_copy(held.at[i], out, out_sem.at[i]))
    for load in loads:
        load.start()
    for i, store in enumerate(stores):
        loads[2 * i].wait()
        loads[2 * i + 1].wait()
        store.start()
    for store in stores:
        store.wait()


def pack(layout, plan, x):
    rows = x.shape[0]
    count = layout.pairs
    return call(
        functools.partial(pack_kernel, layout),
        "pack",
        [f32(rows, 2 * BLK)] * count,
        [SMEM_SPEC, HBM_SPEC],
        [HBM_SPEC] * count,
        [
            pltpu.VMEM((count, rows, 2 * BLK), jnp.float32),
            pltpu.SemaphoreType.DMA((2 * count,)),
            pltpu.SemaphoreType.DMA((count,)),
        ],
        3,
    )(plan, x)


def unpack_kernel(layout, *refs):
    pieces, out_ref, held, in_sem, out_sem = refs[:-4], *refs[-4:]
    width = 2 * BLK
    loads, stores = [], []
    for i, piece in enumerate(pieces):
        start = pl.multiple_of(layout.pair_at(*divmod(i, layout.team)) * width, width)
        loads.append(pltpu.make_async_copy(piece, held.at[i], in_sem.at[i]))
        stores.append(
            pltpu.make_async_copy(held.at[i], out_ref.at[:, pl.ds(start, width)], out_sem.at[i])
        )
    for load in loads:
        load.start()
    for load, store in zip(loads, stores):
        load.wait()
        store.start()
    for store in stores:
        store.wait()


def unpack(layout, pieces):
    rows, width = pieces[0].shape
    count = len(pieces)
    return call(
        functools.partial(unpack_kernel, layout),
        "unpack",
        f32(rows, count * width),
        [HBM_SPEC] * count,
        HBM_SPEC,
        [
            pltpu.VMEM((count, rows, width), jnp.float32),
            pltpu.SemaphoreType.DMA((count,)),
            pltpu.SemaphoreType.DMA((count,)),
        ],
        3,
    )(*pieces)


def gather_terms_kernel(layout, *refs):
    pieces, (upper_ref, lower_ref, terms_ref) = refs[:-3], refs[-3:]
    rows = pieces[0].shape[0]
    for i, piece in enumerate(pieces):
        at = pl.ds(pl.multiple_of(layout.partner(i) * rows, rows), rows)
        upper_ref[at, :] = piece[:, :BLK]
        lower_ref[at, :] = piece[:, BLK:]
    pair_terms(upper_ref, lower_ref, terms_ref)


def gather_terms(layout, pieces):
    tokens = pieces[0].shape[0] * len(pieces)
    return call(
        functools.partial(gather_terms_kernel, layout),
        "gather_terms",
        [f32(tokens, BLK), f32(tokens, BLK), f32(BLK + SQUARES, BLK)],
        [VMEM_SPEC] * len(pieces),
        [VMEM_SPEC] * 3,
        [],
        2,
    )(*pieces)


def choose_terms_kernel(pick_upper, pick_lower, *refs):
    uppers, lowers, (upper_ref, lower_ref, terms_ref) = refs[:2], refs[2:4], refs[4:]
    for pick, choices, out_ref in (
        (pick_upper, uppers, upper_ref),
        (pick_lower, lowers, lower_ref),
    ):
        chosen = pick()

        @pl.when(chosen)
        def _():
            out_ref[...] = choices[0][...]

        @pl.when(jnp.logical_not(chosen))
        def _():
            out_ref[...] = choices[1][...]

    pair_terms(upper_ref, lower_ref, terms_ref)


def choose_terms(picks, uppers, lowers):
    tokens = uppers[0].shape[0]
    return call(
        functools.partial(choose_terms_kernel, *picks),
        "choose_terms",
        [f32(tokens, BLK), f32(tokens, BLK), f32(BLK + SQUARES, BLK)],
        [VMEM_SPEC] * 4,
        [VMEM_SPEC] * 3,
        [],
        2,
    )(*uppers, *lowers)


def total_terms(refs):
    total = refs[0][...]
    for ref in refs[1:]:
        total = total + ref[...]
    return total


def factor_scratch():
    return [pltpu.VMEM((2, BLK, BLK), jnp.float32), pltpu.VMEM((BLK, BLK), jnp.float32)]


def rotate_kernel(upper_ref, lower_ref, *refs):
    terms, (new_upper_ref, new_lower_ref, work_ref, corr_ref) = refs[:-4], refs[-4:]

    def store(at, new_upper, new_lower):
        new_upper_ref[at, :] = new_upper
        new_lower_ref[at, :] = new_lower

    rotated(upper_ref, lower_ref, total_terms(terms), work_ref, corr_ref, store)


def rotate(upper, lower, terms):
    tokens = upper.shape[0]
    return call(
        rotate_kernel,
        "rotate",
        [f32(tokens, BLK), f32(tokens, BLK)],
        [VMEM_SPEC] * (2 + len(terms)),
        [VMEM_SPEC] * 2,
        factor_scratch(),
        15,
    )(upper, lower, *terms)


def rotate_out_kernel(layout, upper_ref, lower_ref, *refs):
    count = layout.team
    terms, refs = refs[: -3 - count], refs[-3 - count :]
    outs, (result_ref, work_ref, corr_ref) = refs[:count], refs[count:]

    def store(at, new_upper, new_lower):
        result_ref[at, :BLK] = new_upper
        result_ref[at, BLK:] = new_lower

    rotated(upper_ref, lower_ref, total_terms(terms), work_ref, corr_ref, store)
    rows = outs[0].shape[0]
    for i, out in enumerate(outs):
        start = pl.multiple_of(layout.partner(i) * rows, rows)
        out[...] = result_ref[pl.ds(start, rows), :]


def rotate_out(layout, upper, lower, terms):
    tokens = upper.shape[0]
    count = layout.team
    return call(
        functools.partial(rotate_out_kernel, layout),
        "rotate_out",
        [f32(tokens // count, 2 * BLK)] * count,
        [VMEM_SPEC] * (2 + len(terms)),
        [VMEM_SPEC] * count,
        [pltpu.VMEM((tokens, 2 * BLK), jnp.float32)] + factor_scratch(),
        15,
    )(upper, lower, *terms)


def on_device(activations, plan):
    token_axes = ("rows", "sub")
    all_axes = ("rows", "cols", "sub")
    layout = Layout(activations.shape[1] // BLK)
    team, teams, held = layout.team, layout.teams, layout.held
    subs, columns, token_group = layout.subs, layout.columns, layout.token_group

    def exchange(pieces):
        arrived = [pieces[0]]
        for shift, piece in zip(layout.shifts[1:], pieces[1:]):
            route = [(t, t ^ shift) for t in range(token_group)]
            arrived.append(lax.ppermute(piece, token_axes, route))
        return arrived

    def shared(terms):
        gathered = [terms]
        for step in range(1, teams):
            route = [(t, (t + step * team) % token_group) for t in range(token_group)]
            gathered.append(lax.ppermute(terms, token_axes, route))
        return gathered

    def along(block, distance):
        route = []
        for at in range(columns * team):
            if 0 <= at + distance < columns * team:
                for group in range(teams):
                    ends = []
                    for one in (at, at + distance):
                        home, inner = divmod(one, team)
                        inner = team - 1 - inner if home % 2 else inner
                        row, sub = divmod(group * team + inner, subs)
                        ends.append((row * columns + home) * subs + sub)
                    route.append(tuple(ends))
        return lax.ppermute(block, all_axes, route)

    def always():
        return lax.axis_index("cols") >= 0

    pieces = pack(layout, plan, activations)
    arrived = [exchange(pieces[g * team : (g + 1) * team]) for g in range(held)]
    ready = [gather_terms(layout, piece) for piece in arrived]
    summed = [shared(terms) for _, _, terms in ready]
    blocks = [rotate(ready[g][0], ready[g][1], summed[g]) for g in range(held)]

    top_upper, top_lower = blocks[-1]
    if held == 1:
        top_upper = jnp.where(layout.first(), top_lower, top_upper)
    leaving = along(blocks[0][1], -1)
    arriving = along(top_upper, 1)

    results = [None] * held
    ready = [None] * held
    for g in reversed(range(held)):
        if g == 0:
            uppers, pick_upper = (blocks[0][0], arriving), layout.first
        elif g == 1:
            uppers, pick_upper = (blocks[0][1], blocks[0][0]), layout.first
        else:
            uppers, pick_upper = (blocks[g - 1][0],) * 2, always
        if g == held - 1:
            lowers, pick_lower = (blocks[g][0], leaving), layout.final
        else:
            lowers, pick_lower = (blocks[g + 1][1],) * 2, always
        ready[g] = choose_terms((pick_upper, pick_lower), uppers, lowers)
    for g in reversed(range(held)):
        upper, lower, terms = ready[g]
        results[g] = exchange(rotate_out(layout, upper, lower, shared(terms)))
    return unpack(layout, [piece for result in results for piece in result])


def solution(mesh):
    in_specs = (P(("groups", "rows", "sub"), "cols"), P())
    out_specs = P(("groups", "rows", "sub"), "cols")
    return jax.shard_map(
        on_device, mesh=mesh, in_specs=in_specs, out_specs=out_specs, check_vma=False
    )
```

```python
import functools

import jax
import jax.numpy as jnp
from jax import lax
from jax.experimental import pallas as pl
from jax.experimental.pallas import tpu as pltpu
from jax.sharding import PartitionSpec as P

BLK = 256
ROUNDS = 2
PANEL = 64
SUBLANES = 8

epsilon = 1e-06
HIGH = lax.Precision.HIGHEST
VMEM_LIMIT = 16 * 1024 * 1024
TEAM_CHIPS = 2
SQUARES = 8
CHUNK = 256


def contract(a, b, a_dim, b_dim):
    return lax.dot_general(
        a, b, (((a_dim,), (b_dim,)), ((), ())), precision=HIGH, preferred_element_type=jnp.float32
    )


def iota2(shape, dim):
    return lax.broadcasted_iota(jnp.int32, shape, dim)


def reciprocal(x):
    guess = pl.reciprocal(x, approx=True)
    return guess * (2.0 - x * guess)


def eliminate(blocks):
    width = 2 * PANEL
    shape = (SUBLANES, width)
    tiles = PANEL // SUBLANES
    lines = range(SUBLANES)
    ident = jnp.where(
        iota2((PANEL, width), 0) == lax.rem(iota2((PANEL, width), 1), PANEL), 1.0, 0.0
    ).astype(jnp.float32)
    sub = iota2(shape, 0)
    halves = jnp.where(iota2(shape, 1) < PANEL, 0, PANEL)
    whole = jnp.concatenate(blocks, axis=1)
    parts = [whole[SUBLANES * v : SUBLANES * (v + 1)] for v in range(tiles)]
    sides = [ident[SUBLANES * v : SUBLANES * (v + 1)] for v in range(tiles)]
    outs = []

    def spread(tile, line):
        return jnp.broadcast_to(tile[line : line + 1, :], shape)

    for q in range(tiles):
        columns = [
            [
                jnp.take_along_axis(parts[v], halves + (SUBLANES * q + j), axis=1)
                for j in lines
            ]
            for v in range(q, tiles)
        ]
        entry = [[spread(columns[0][j], i) for j in range(i + 1)] for i in lines]
        rows = [spread(parts[q], i) for i in lines]
        side_rows = [spread(sides[q], i) for i in lines]
        inverses = []
        for s in lines:
            inverse = reciprocal(entry[s][s])
            inverses.append(inverse)
            factors = {i: entry[i][s] * inverse for i in range(s + 1, SUBLANES)}
            for i in range(s + 1, SUBLANES):
                for j in range(s + 1, i + 1):
                    entry[i][j] = entry[i][j] - factors[i] * entry[j][s]
            for i in range(s + 1, SUBLANES):
                rows[i] = rows[i] - factors[i] * rows[s]
                side_rows[i] = side_rows[i] - factors[i] * side_rows[s]
        for v in range(q + 1, tiles):
            factors = []
            for s in lines:
                value = columns[v - q][s]
                for t in range(s):
                    value = value - factors[t] * entry[s][t]
                factors.append(value * inverses[s])
            for s in lines:
                parts[v] = parts[v] - factors[s] * rows[s]
                sides[v] = sides[v] - factors[s] * side_rows[s]
        tile = side_rows[0] * lax.rsqrt(entry[0][0])
        for i in lines[1:]:
            tile = jnp.where(sub == i, side_rows[i] * lax.rsqrt(entry[i][i]), tile)
        outs.append(tile)
    out = jnp.concatenate(outs, axis=0)
    return out[:, :PANEL], out[:, PANEL:]


def inverse_factors(work_ref, inv_ref):
    inv_ref[...] = jnp.zeros_like(inv_ref)
    ident = jnp.where(iota2((PANEL, PANEL), 0) == iota2((PANEL, PANEL), 1), 1.0, 0.0).astype(jnp.float32)
    for p in range(BLK // PANEL):
        top = p * PANEL
        end = top + PANEL
        invs = eliminate([work_ref[m, top:end, top:end] for m in range(2)])
        for m in range(2):
            work_ref[m, top:end, top:end] = ident
            rows = contract(invs[m], work_ref[m, top:end, :], 1, 0)
            inv_ref[m, top:end, :end] = rows[:, :end]
            if end < BLK:
                work_ref[m, end:, top:end] = jnp.zeros((BLK - end, PANEL), jnp.float32)
                work_ref[m, end:, :] = work_ref[m, end:, :] - contract(rows[:, end:], rows, 0, 0)


def pair_terms(blocks_ref, terms_ref):
    tokens = blocks_ref.shape[1]
    chunk = min(CHUNK, tokens)
    line = iota2((SQUARES, BLK), 0)
    terms_ref[...] = jnp.zeros_like(terms_ref)

    def step(i, _):
        at = pl.ds(pl.multiple_of(i * chunk, chunk), chunk)
        upper, lower = blocks_ref[0, at, :], blocks_ref[1, at, :]
        upper_sq = jnp.sum(upper * upper, axis=0, keepdims=True)
        lower_sq = jnp.sum(lower * lower, axis=0, keepdims=True)
        squares = jnp.where(line == 0, upper_sq, jnp.where(line == 1, lower_sq, 0.0))
        terms_ref[:BLK] += contract(upper, lower, 0, 0)
        terms_ref[BLK:] += squares
        return 0

    lax.fori_loop(0, tokens // chunk, step, 0)


SMEM_SPEC = pl.BlockSpec(memory_space=pltpu.SMEM)
VMEM_SPEC = pl.BlockSpec(memory_space=pltpu.VMEM)
HBM_SPEC = pl.BlockSpec(memory_space=pltpu.HBM)


def call(kernel, name, out_shape, in_specs, out_specs, scratch, micros):
    return pl.pallas_call(
        kernel,
        out_shape=out_shape,
        in_specs=in_specs,
        out_specs=out_specs,
        scratch_shapes=scratch,
        compiler_params=pltpu.CompilerParams(vmem_limit_bytes=VMEM_LIMIT),
        cost_estimate=pl.CostEstimate(
            flops=int(micros * 1e9), bytes_accessed=1 << 20, transcendentals=0
        ),
        name=name,
    )


def f32(*shape):
    return jax.ShapeDtypeStruct(shape, jnp.float32)


class Layout:
    def __init__(self, block_count):
        self.block_count = block_count
        self.pairs = block_count // 2
        self.subs = lax.axis_size("sub")
        self.columns = lax.axis_size("cols")
        self.token_group = lax.axis_size("rows") * self.subs
        self.team = min(self.pairs, TEAM_CHIPS * self.subs, self.token_group)
        self.teams = self.token_group // self.team
        self.held = self.pairs // self.team
        assert self.team * self.teams == self.token_group
        assert self.team * self.held == self.pairs and self.team & (self.team - 1) == 0
        self.shifts = [0] + list(range(self.team - 1, 0, -1))

    def member(self):
        return lax.rem(lax.axis_index("rows") * self.subs + lax.axis_index("sub"), self.team)

    def partner(self, i):
        return lax.bitwise_xor(self.member(), jnp.int32(self.shifts[i]))

    def place_of(self, member):
        backwards = lax.rem(lax.axis_index("cols"), 2) == 1
        return jnp.where(backwards, self.team - 1 - member, member)

    def pair_at(self, g, i):
        return self.place_of(self.partner(i)) * self.held + g

    def first(self):
        return jnp.logical_and(lax.axis_index("cols") == 0, self.place_of(self.member()) == 0)

    def final(self):
        return jnp.logical_and(
            lax.axis_index("cols") == self.columns - 1,
            self.place_of(self.member()) == self.team - 1,
        )


def pack_kernel(layout, plan_ref, x_ref, *refs):
    outs, held, in_sem, out_sem = refs[:-3], *refs[-3:]
    base = lax.axis_index("cols") * layout.block_count
    loads, stores = [], []
    for i, out in enumerate(outs):
        pair = layout.pair_at(*divmod(i, layout.team))
        for half in range(2):
            block = plan_ref[0, base + 2 * pair + half] - base
            start = pl.multiple_of(block * BLK, BLK)
            loads.append(
                pltpu.make_async_copy(
                    x_ref.at[:, pl.ds(start, BLK)],
                    held.at[i, :, half * BLK : (half + 1) * BLK],
                    in_sem.at[2 * i + half],
                )
            )
        stores.append(pltpu.make_async_copy(held.at[i], out, out_sem.at[i]))
    for load in loads:
        load.start()
    for i, store in enumerate(stores):
        loads[2 * i].wait()
        loads[2 * i + 1].wait()
        store.start()
    for store in stores:
        store.wait()


def pack(layout, plan, x):
    rows = x.shape[0]
    count = layout.pairs
    return call(
        functools.partial(pack_kernel, layout),
        "pack",
        [f32(rows, 2 * BLK)] * count,
        [SMEM_SPEC, HBM_SPEC],
        [HBM_SPEC] * count,
        [
            pltpu.VMEM((count, rows, 2 * BLK), jnp.float32),
            pltpu.SemaphoreType.DMA((2 * count,)),
            pltpu.SemaphoreType.DMA((count,)),
        ],
        3,
    )(plan, x)


def unpack_kernel(layout, *refs):
    pieces, out_ref, held, in_sem, out_sem = refs[:-4], *refs[-4:]
    width = 2 * BLK
    loads, stores = [], []
    for i, piece in enumerate(pieces):
        start = pl.multiple_of(layout.pair_at(*divmod(i, layout.team)) * width, width)
        loads.append(pltpu.make_async_copy(piece, held.at[i], in_sem.at[i]))
        stores.append(
            pltpu.make_async_copy(held.at[i], out_ref.at[:, pl.ds(start, width)], out_sem.at[i])
        )
    for load in loads:
        load.start()
    for load, store in zip(loads, stores):
        load.wait()
        store.start()
    for store in stores:
        store.wait()


def unpack(layout, pieces):
    rows, width = pieces[0].shape
    count = len(pieces)
    return call(
        functools.partial(unpack_kernel, layout),
        "unpack",
        f32(rows, count * width),
        [HBM_SPEC] * count,
        HBM_SPEC,
        [
            pltpu.VMEM((count, rows, width), jnp.float32),
            pltpu.SemaphoreType.DMA((count,)),
            pltpu.SemaphoreType.DMA((count,)),
        ],
        3,
    )(*pieces)


def gather_terms_kernel(layout, *refs):
    pieces, (blocks_ref, terms_ref) = refs[:-2], refs[-2:]
    rows = pieces[0].shape[0]
    for i, piece in enumerate(pieces):
        at = pl.ds(pl.multiple_of(layout.partner(i) * rows, rows), rows)
        blocks_ref[0, at, :] = piece[:, :BLK]
        blocks_ref[1, at, :] = piece[:, BLK:]
    pair_terms(blocks_ref, terms_ref)


def gather_terms(layout, pieces):
    tokens = pieces[0].shape[0] * len(pieces)
    return call(
        functools.partial(gather_terms_kernel, layout),
        "gather_terms",
        [f32(2, tokens, BLK), f32(BLK + SQUARES, BLK)],
        [VMEM_SPEC] * len(pieces),
        [VMEM_SPEC] * 2,
        [],
        2,
    )(*pieces)


def choose_terms_kernel(pick_upper, pick_lower, uppers, lowers, *refs):
    inputs, (blocks_ref, terms_ref) = refs[:-2], refs[-2:]

    def fetch(m, at):
        if len(at) == 1:
            blocks_ref[m] = inputs[at[0]][...]
        else:
            pair_ref, turn_ref, inv_ref = (inputs[i] for i in at)
            chunk = min(CHUNK, pair_ref.shape[1])

            def step(i, _):
                rows = pl.ds(pl.multiple_of(i * chunk, chunk), chunk)
                blocks_ref[m, rows, :] = turned(pair_ref, turn_ref, inv_ref, 0, rows)
                return 0

            lax.fori_loop(0, pair_ref.shape[1] // chunk, step, 0)

    for m, (pick, choices) in enumerate(((pick_upper, uppers), (pick_lower, lowers))):
        chosen = pick()
        pl.when(chosen)(functools.partial(fetch, m, choices[0]))
        pl.when(jnp.logical_not(chosen))(functools.partial(fetch, m, choices[1]))
    pair_terms(blocks_ref, terms_ref)


def choose_terms(picks, uppers, lowers):
    tokens = uppers[0][0].shape[-2]
    inputs, places = [], []
    for choice in (*uppers, *lowers):
        places.append(tuple(range(len(inputs), len(inputs) + len(choice))))
        inputs.extend(choice)
    return call(
        functools.partial(choose_terms_kernel, *picks, places[:2], places[2:]),
        "choose_terms",
        [f32(2, tokens, BLK), f32(BLK + SQUARES, BLK)],
        [VMEM_SPEC] * len(inputs),
        [VMEM_SPEC] * 2,
        [],
        2,
    )(*inputs)


def total_terms(refs):
    total = refs[0][...]
    for ref in refs[1:]:
        total = total + ref[...]
    return total


def factor_kernel(*refs):
    terms, (turn_ref, inv_ref, work_ref) = refs[:-3], refs[-3:]
    terms = total_terms(terms)
    square = (BLK, BLK)
    diagonal = iota2(square, 0) == iota2(square, 1)
    ident = jnp.where(diagonal, 1.0, 0.0).astype(jnp.float32)
    upper_sq, lower_sq = terms[BLK : BLK + 1], terms[BLK + 1 : BLK + 2]
    upper_sq = jnp.sum(
        jnp.where(diagonal, jnp.broadcast_to(upper_sq, square), 0.0), axis=1, keepdims=True
    )
    corr = terms[:BLK] * lax.rsqrt(upper_sq + epsilon) * lax.rsqrt(lower_sq + epsilon)
    turn_ref[0] = corr
    turn_ref[1] = -jnp.transpose(corr)
    for m in range(2):
        work_ref[m] = ident + contract(turn_ref[m], turn_ref[m], 1, 1)
    inverse_factors(work_ref, inv_ref)


def factor(terms):
    return call(
        factor_kernel,
        "factor",
        [f32(2, BLK, BLK), f32(2, BLK, BLK)],
        [VMEM_SPEC] * len(terms),
        [VMEM_SPEC] * 2,
        [pltpu.VMEM((2, BLK, BLK), jnp.float32)],
        11,
    )(*terms)


def turned(blocks_ref, turn_ref, inv_ref, m, at):
    mixed = blocks_ref[m, at, :] + contract(blocks_ref[1 - m, at, :], turn_ref[m], 1, 1)
    return contract(mixed, inv_ref[m], 1, 1)


def apply_rotation(blocks_ref, turn_ref, inv_ref, out_ref):
    tokens = blocks_ref.shape[1]
    chunk = min(CHUNK, tokens)
    count = tokens // chunk

    def step(i, _):
        m = i // count
        at = pl.ds(pl.multiple_of(lax.rem(i, count) * chunk, chunk), chunk)
        out_ref[m, at, :] = turned(blocks_ref, turn_ref, inv_ref, m, at)
        return 0

    lax.fori_loop(0, 2 * count, step, 0)


def turn_kernel(blocks_ref, turn_ref, inv_ref, upper_ref, lower_ref, out_ref):
    apply_rotation(blocks_ref, turn_ref, inv_ref, out_ref)
    upper_ref[...] = out_ref[0]
    lower_ref[...] = out_ref[1]


def turn(blocks, factors):
    tokens = blocks.shape[1]
    return call(
        turn_kernel,
        "turn",
        [f32(tokens, BLK)] * 2,
        [VMEM_SPEC] * 3,
        [VMEM_SPEC] * 2,
        [pltpu.VMEM((2, tokens, BLK), jnp.float32)],
        4,
    )(blocks, *factors)


def turn_out_kernel(layout, blocks_ref, turn_ref, inv_ref, *refs):
    outs, out_ref = refs[:-1], refs[-1]
    apply_rotation(blocks_ref, turn_ref, inv_ref, out_ref)
    rows = outs[0].shape[0]
    for i, out in enumerate(outs):
        at = pl.ds(pl.multiple_of(layout.partner(i) * rows, rows), rows)
        out[:, :BLK] = out_ref[0, at, :]
        out[:, BLK:] = out_ref[1, at, :]


def turn_out(layout, blocks, factors):
    tokens = blocks.shape[1]
    count = layout.team
    return call(
        functools.partial(turn_out_kernel, layout),
        "turn_out",
        [f32(tokens // count, 2 * BLK)] * count,
        [VMEM_SPEC] * 3,
        [VMEM_SPEC] * count,
        [pltpu.VMEM((2, tokens, BLK), jnp.float32)],
        4,
    )(blocks, *factors)


def on_device(activations, plan):
    token_axes = ("rows", "sub")
    all_axes = ("rows", "cols", "sub")
    layout = Layout(activations.shape[1] // BLK)
    team, teams, held = layout.team, layout.teams, layout.held
    subs, columns, token_group = layout.subs, layout.columns, layout.token_group

    def exchange(pieces):
        arrived = [pieces[0]]
        for shift, piece in zip(layout.shifts[1:], pieces[1:]):
            route = [(t, t ^ shift) for t in range(token_group)]
            arrived.append(lax.ppermute(piece, token_axes, route))
        return arrived

    def shared(terms):
        gathered = [terms]
        for step in range(1, teams):
            route = [(t, (t + step * team) % token_group) for t in range(token_group)]
            gathered.append(lax.ppermute(terms, token_axes, route))
        return gathered

    def along(block, distance):
        route = []
        for at in range(columns * team):
            if 0 <= at + distance < columns * team:
                for group in range(teams):
                    ends = []
                    for one in (at, at + distance):
                        home, inner = divmod(one, team)
                        inner = team - 1 - inner if home % 2 else inner
                        row, sub = divmod(group * team + inner, subs)
                        ends.append((row * columns + home) * subs + sub)
                    route.append(tuple(ends))
        return lax.ppermute(block, all_axes, route)

    def always():
        return lax.axis_index("cols") >= 0

    pieces = pack(layout, plan, activations)
    pieces = [pieces[g * team : (g + 1) * team] for g in range(held)]
    arrived = []
    for piece in pieces:
        if arrived:
            piece, arrived[-1] = lax.optimization_barrier((piece, arrived[-1]))
        arrived.append(exchange(piece))
    ready = [gather_terms(layout, piece) for piece in arrived]
    summed = [shared(terms) for _, terms in ready]

    top = held - 1

    def next_terms(g, done, edge, leaving, arriving):
        if g == 0:
            uppers, pick_upper = ([done[0][0]], [arriving]), layout.first
        elif g == 1:
            uppers, pick_upper = ([done[0][1]], [done[0][0]]), layout.first
        else:
            uppers, pick_upper = ([done[g - 1][0]],) * 2, always
        if g == top:
            lowers, pick_lower = (edge, [leaving]), layout.final
        else:
            lowers, pick_lower = ([done[g + 1][1]],) * 2, always
        return choose_terms((pick_upper, pick_lower), uppers, lowers)

    done, nexts = [], [None] * held
    for g in range(top):
        done.append(turn(ready[g][0], factor(summed[g])))
    factors = factor(summed[top])
    if top:
        leaving = along(done[0][1], -1)
        blocks, terms = next_terms(top, done, [ready[top][0], *factors], leaving, None)
        nexts[top] = (blocks, shared(terms))
        factors, _ = lax.optimization_barrier((factors, terms))
    done.append(turn(ready[top][0], factors))
    if not top:
        leaving = along(done[0][1], -1)
    last_upper = done[top][0]
    if not top:
        last_upper = jnp.where(layout.first(), done[top][1], last_upper)
    arriving = along(last_upper, 1)
    for g in reversed(range(held)):
        if nexts[g] is None:
            blocks, terms = next_terms(g, done, [done[top][0]], leaving, arriving)
            nexts[g] = (blocks, shared(terms))

    results = [None] * held
    for g in reversed(range(held)):
        blocks, terms = nexts[g]
        results[g] = exchange(turn_out(layout, blocks, factor(terms)))
    return unpack(layout, [piece for result in results for piece in result])


def solution(mesh):
    in_specs = (P(("groups", "rows", "sub"), "cols"), P())
    out_specs = P(("groups", "rows", "sub"), "cols")
    return jax.shard_map(
        on_device, mesh=mesh, in_specs=in_specs, out_specs=out_specs, check_vma=False
    )
```

```python
import functools

import jax
import jax.numpy as jnp
from jax import lax
from jax.experimental import pallas as pl
from jax.experimental.pallas import tpu as pltpu
from jax.sharding import PartitionSpec as P

BLK = 256
ROUNDS = 2
PANEL = 64
SUBLANES = 8

epsilon = 1e-06
HIGH = lax.Precision.HIGHEST
VMEM_LIMIT = 16 * 1024 * 1024
PACK_VMEM_LIMIT = 61 * 1024 * 1024
TEAM_CHIPS = 2
SQUARES = 8
CHUNK = 256


def contract(a, b, a_dim, b_dim):
    return lax.dot_general(
        a, b, (((a_dim,), (b_dim,)), ((), ())), precision=HIGH, preferred_element_type=jnp.float32
    )


def iota2(shape, dim):
    return lax.broadcasted_iota(jnp.int32, shape, dim)


def reciprocal(x):
    guess = pl.reciprocal(x, approx=True)
    return guess, 2.0 - x * guess


def eliminate(blocks):
    width = 2 * PANEL
    shape = (SUBLANES, width)
    tiles = PANEL // SUBLANES
    lines = range(SUBLANES)
    ident = jnp.where(
        iota2((PANEL, width), 0) == lax.rem(iota2((PANEL, width), 1), PANEL), 1.0, 0.0
    ).astype(jnp.float32)
    sub = iota2(shape, 0)
    halves = jnp.where(iota2(shape, 1) < PANEL, 0, PANEL)
    whole = jnp.concatenate(blocks, axis=1)
    parts = [whole[SUBLANES * v : SUBLANES * (v + 1)] for v in range(tiles)]
    sides = [ident[SUBLANES * v : SUBLANES * (v + 1)] for v in range(tiles)]
    outs = []

    def spread(tile, line):
        return jnp.broadcast_to(tile[line : line + 1, :], shape)

    for q in range(tiles):
        columns = [
            [
                jnp.take_along_axis(parts[v], halves + (SUBLANES * q + j), axis=1)
                for j in lines
            ]
            for v in range(q, tiles)
        ]
        entry = [[spread(columns[0][j], i) for j in range(i + 1)] for i in lines]
        rows = [spread(parts[q], i) for i in lines]
        side_rows = [spread(sides[q], i) for i in lines]
        inverses = []
        for s in lines:
            guess, mend = reciprocal(entry[s][s])
            inverses.append(guess * mend)
            factors = {i: (entry[i][s] * guess) * mend for i in range(s + 1, SUBLANES)}
            for i in range(s + 1, SUBLANES):
                for j in range(s + 1, i + 1):
                    entry[i][j] = entry[i][j] - factors[i] * entry[j][s]
            for i in range(s + 1, SUBLANES):
                rows[i] = rows[i] - factors[i] * rows[s]
                side_rows[i] = side_rows[i] - factors[i] * side_rows[s]
        for v in range(q + 1, tiles):
            factors = []
            for s in lines:
                value = columns[v - q][s]
                for t in range(s):
                    value = value - factors[t] * entry[s][t]
                factors.append(value * inverses[s])
            for s in lines:
                parts[v] = parts[v] - factors[s] * rows[s]
                sides[v] = sides[v] - factors[s] * side_rows[s]
        tile = side_rows[0] * lax.rsqrt(entry[0][0])
        for i in lines[1:]:
            tile = jnp.where(sub == i, side_rows[i] * lax.rsqrt(entry[i][i]), tile)
        outs.append(tile)
    out = jnp.concatenate(outs, axis=0)
    return out[:, :PANEL], out[:, PANEL:]


def inverse_factors(work_ref, inv_ref):
    inv_ref[:, :, :BLK] = jnp.zeros((2, BLK, BLK), jnp.float32)
    ident = jnp.where(iota2((PANEL, PANEL), 0) == iota2((PANEL, PANEL), 1), 1.0, 0.0).astype(jnp.float32)
    for p in range(BLK // PANEL):
        top = p * PANEL
        end = top + PANEL
        invs = eliminate([work_ref[m, top:end, top:end] for m in range(2)])
        for m in range(2):
            work_ref[m, top:end, top:end] = ident
            rows = contract(invs[m], work_ref[m, top:end, :], 1, 0)
            inv_ref[m, top:end, :end] = rows[:, :end]
            inv_ref[m, top:end, BLK:] = rows[:, BLK:]
            if end < BLK:
                work_ref[m, end:, top:end] = jnp.zeros((BLK - end, PANEL), jnp.float32)
                work_ref[m, end:, :] = work_ref[m, end:, :] - contract(rows[:, end:BLK], rows, 0, 0)


def pair_terms(blocks_ref, terms_ref):
    tokens = blocks_ref.shape[1]
    chunk = min(CHUNK, tokens)
    line = iota2((SQUARES, BLK), 0)
    terms_ref[...] = jnp.zeros_like(terms_ref)

    def step(i, _):
        at = pl.ds(pl.multiple_of(i * chunk, chunk), chunk)
        upper, lower = blocks_ref[0, at, :], blocks_ref[1, at, :]
        upper_sq = jnp.sum(upper * upper, axis=0, keepdims=True)
        lower_sq = jnp.sum(lower * lower, axis=0, keepdims=True)
        squares = jnp.where(line == 0, upper_sq, jnp.where(line == 1, lower_sq, 0.0))
        terms_ref[:BLK] += contract(upper, lower, 0, 0)
        terms_ref[BLK:] += squares
        return 0

    lax.fori_loop(0, tokens // chunk, step, 0)


SMEM_SPEC = pl.BlockSpec(memory_space=pltpu.SMEM)
VMEM_SPEC = pl.BlockSpec(memory_space=pltpu.VMEM)
HBM_SPEC = pl.BlockSpec(memory_space=pltpu.HBM)


def call(kernel, name, out_shape, in_specs, out_specs, scratch, micros, vmem=VMEM_LIMIT):
    return pl.pallas_call(
        kernel,
        out_shape=out_shape,
        in_specs=in_specs,
        out_specs=out_specs,
        scratch_shapes=scratch,
        compiler_params=pltpu.CompilerParams(vmem_limit_bytes=vmem),
        cost_estimate=pl.CostEstimate(
            flops=int(micros * 1e9), bytes_accessed=1 << 20, transcendentals=0
        ),
        name=name,
    )


def f32(*shape):
    return jax.ShapeDtypeStruct(shape, jnp.float32)


class Layout:
    def __init__(self, block_count):
        self.block_count = block_count
        self.pairs = block_count // 2
        self.subs = lax.axis_size("sub")
        self.columns = lax.axis_size("cols")
        self.token_group = lax.axis_size("rows") * self.subs
        self.team = min(self.pairs, TEAM_CHIPS * self.subs, self.token_group)
        self.teams = self.token_group // self.team
        self.held = self.pairs // self.team
        assert self.team * self.teams == self.token_group
        assert self.team * self.held == self.pairs and self.team & (self.team - 1) == 0
        self.shifts = [0] + list(range(self.team - 1, 0, -1))

    def member(self):
        return lax.rem(lax.axis_index("rows") * self.subs + lax.axis_index("sub"), self.team)

    def partner(self, i):
        return lax.bitwise_xor(self.member(), jnp.int32(self.shifts[i]))

    def place_of(self, member):
        backwards = lax.rem(lax.axis_index("cols"), 2) == 1
        return jnp.where(backwards, self.team - 1 - member, member)

    def pair_at(self, g, i):
        return self.place_of(self.partner(i)) * self.held + g

    def first(self):
        return jnp.logical_and(lax.axis_index("cols") == 0, self.place_of(self.member()) == 0)

    def final(self):
        return jnp.logical_and(
            lax.axis_index("cols") == self.columns - 1,
            self.place_of(self.member()) == self.team - 1,
        )


def pack_kernel(layout, plan_ref, x_ref, *refs):
    outs, in_sem = refs[:-1], refs[-1]
    base = lax.axis_index("cols") * layout.block_count
    loads = []
    for i, out in enumerate(outs):
        pair = layout.pair_at(*divmod(i, layout.team))
        for half in range(2):
            block = plan_ref[0, base + 2 * pair + half] - base
            start = pl.multiple_of(block * BLK, BLK)
            loads.append(
                pltpu.make_async_copy(
                    x_ref.at[:, pl.ds(start, BLK)],
                    out.at[:, half * BLK : (half + 1) * BLK],
                    in_sem.at[2 * i + half],
                )
            )
    for load in loads:
        load.start()
    for load in loads:
        load.wait()


def pack(layout, plan, x):
    rows = x.shape[0]
    count = layout.pairs
    return call(
        functools.partial(pack_kernel, layout),
        "pack",
        [f32(rows, 2 * BLK)] * count,
        [SMEM_SPEC, HBM_SPEC],
        [VMEM_SPEC] * count,
        [pltpu.SemaphoreType.DMA((2 * count,))],
        3,
        PACK_VMEM_LIMIT,
    )(plan, x)


def unpack_kernel(layout, *refs):
    pieces, out_ref, held, in_sem, out_sem = refs[:-4], *refs[-4:]
    width = 2 * BLK
    loads, stores = [], []
    for i, piece in enumerate(pieces):
        start = pl.multiple_of(layout.pair_at(*divmod(i, layout.team)) * width, width)
        loads.append(pltpu.make_async_copy(piece, held.at[i], in_sem.at[i]))
        stores.append(
            pltpu.make_async_copy(held.at[i], out_ref.at[:, pl.ds(start, width)], out_sem.at[i])
        )
    for load in loads:
        load.start()
    for load, store in zip(loads, stores):
        load.wait()
        store.start()
    for store in stores:
        store.wait()


def unpack(layout, pieces):
    rows, width = pieces[0].shape
    count = len(pieces)
    return call(
        functools.partial(unpack_kernel, layout),
        "unpack",
        f32(rows, count * width),
        [HBM_SPEC] * count,
        HBM_SPEC,
        [
            pltpu.VMEM((count, rows, width), jnp.float32),
            pltpu.SemaphoreType.DMA((count,)),
            pltpu.SemaphoreType.DMA((count,)),
        ],
        3,
    )(*pieces)


def gather_terms_kernel(layout, *refs):
    pieces, (blocks_ref, terms_ref) = refs[:-2], refs[-2:]
    rows = pieces[0].shape[0]
    for i, piece in enumerate(pieces):
        at = pl.ds(pl.multiple_of(layout.partner(i) * rows, rows), rows)
        blocks_ref[0, at, :] = piece[:, :BLK]
        blocks_ref[1, at, :] = piece[:, BLK:]
    pair_terms(blocks_ref, terms_ref)


def gather_terms(layout, pieces):
    tokens = pieces[0].shape[0] * len(pieces)
    return call(
        functools.partial(gather_terms_kernel, layout),
        "gather_terms",
        [f32(2, tokens, BLK), f32(BLK + SQUARES, BLK)],
        [VMEM_SPEC] * len(pieces),
        [VMEM_SPEC] * 2,
        [],
        2,
    )(*pieces)


def choose_terms_kernel(pick_upper, pick_lower, uppers, lowers, *refs):
    inputs, (blocks_ref, terms_ref) = refs[:-2], refs[-2:]

    def fetch(m, at):
        if len(at) == 1:
            blocks_ref[m] = inputs[at[0]][...]
        else:
            pair_ref, inv_ref = (inputs[i] for i in at)
            chunk = min(CHUNK, pair_ref.shape[1])

            def step(i, _):
                rows = pl.ds(pl.multiple_of(i * chunk, chunk), chunk)
                blocks_ref[m, rows, :] = turned(pair_ref[0, rows, :], pair_ref[1, rows, :], inv_ref, 0)
                return 0

            lax.fori_loop(0, pair_ref.shape[1] // chunk, step, 0)

    for m, (pick, choices) in enumerate(((pick_upper, uppers), (pick_lower, lowers))):
        chosen = pick()
        pl.when(chosen)(functools.partial(fetch, m, choices[0]))
        pl.when(jnp.logical_not(chosen))(functools.partial(fetch, m, choices[1]))
    pair_terms(blocks_ref, terms_ref)


def choose_terms(picks, uppers, lowers):
    tokens = uppers[0][0].shape[-2]
    inputs, places = [], []
    for choice in (*uppers, *lowers):
        places.append(tuple(range(len(inputs), len(inputs) + len(choice))))
        inputs.extend(choice)
    return call(
        functools.partial(choose_terms_kernel, *picks, places[:2], places[2:]),
        "choose_terms",
        [f32(2, tokens, BLK), f32(BLK + SQUARES, BLK)],
        [VMEM_SPEC] * len(inputs),
        [VMEM_SPEC] * 2,
        [],
        2,
    )(*inputs)


def total_terms(refs):
    total = refs[0][...]
    for ref in refs[1:]:
        total = total + ref[...]
    return total


def factor_kernel(*refs):
    terms, (inv_ref, work_ref) = refs[:-2], refs[-2:]
    terms = total_terms(terms)
    square = (BLK, BLK)
    diagonal = iota2(square, 0) == iota2(square, 1)
    ident = jnp.where(diagonal, 1.0, 0.0).astype(jnp.float32)
    upper_sq, lower_sq = terms[BLK : BLK + 1], terms[BLK + 1 : BLK + 2]
    upper_sq = jnp.sum(
        jnp.where(diagonal, jnp.broadcast_to(upper_sq, square), 0.0), axis=1, keepdims=True
    )
    corr = terms[:BLK] * lax.rsqrt(upper_sq + epsilon) * lax.rsqrt(lower_sq + epsilon)
    work_ref[0, :, BLK:] = corr
    work_ref[1, :, BLK:] = -jnp.transpose(corr)
    for m in range(2):
        work_ref[m, :, :BLK] = ident + contract(work_ref[m, :, BLK:], work_ref[m, :, BLK:], 1, 1)
    inverse_factors(work_ref, inv_ref)


def factor(terms):
    return call(
        factor_kernel,
        "factor",
        f32(2, BLK, 2 * BLK),
        [VMEM_SPEC] * len(terms),
        VMEM_SPEC,
        [pltpu.VMEM((2, BLK, 2 * BLK), jnp.float32)],
        11,
    )(*terms)


def turned(own, other, inv_ref, m):
    return contract(own, inv_ref[m, :, :BLK], 1, 1) + contract(other, inv_ref[m, :, BLK:], 1, 1)


def turn_kernel(m, blocks_ref, inv_ref, out_ref):
    out_ref[...] = turned(blocks_ref[m], blocks_ref[1 - m], inv_ref, m)


def turn(m, blocks, factors):
    return call(
        functools.partial(turn_kernel, m),
        "turn",
        f32(blocks.shape[1], BLK),
        [VMEM_SPEC] * 2,
        VMEM_SPEC,
        [],
        2,
    )(blocks, factors)


def turn_out_kernel(layout, partners, blocks_ref, inv_ref, *refs):
    outs, out_ref = refs[:-1], refs[-1]
    rows = outs[0].shape[0]
    spans = [pl.ds(pl.multiple_of(layout.partner(i) * rows, rows), rows) for i in partners]

    def step(m, _):
        own = jnp.concatenate([blocks_ref[m, at, :] for at in spans], axis=0)
        other = jnp.concatenate([blocks_ref[1 - m, at, :] for at in spans], axis=0)
        out_ref[m] = turned(own, other, inv_ref, m)
        return 0

    lax.fori_loop(0, 2, step, 0)
    for i, out in enumerate(outs):
        out[:, :BLK] = out_ref[0, i * rows : (i + 1) * rows, :]
        out[:, BLK:] = out_ref[1, i * rows : (i + 1) * rows, :]


def turn_out(layout, partners, blocks, factors):
    rows = blocks.shape[1] // layout.team
    count = len(partners)
    return call(
        functools.partial(turn_out_kernel, layout, partners),
        "turn_out",
        [f32(rows, 2 * BLK)] * count,
        [VMEM_SPEC] * 2,
        [VMEM_SPEC] * count,
        [pltpu.VMEM((2, rows * count, BLK), jnp.float32)],
        2,
    )(blocks, factors)


def on_device(activations, plan):
    token_axes = ("rows", "sub")
    all_axes = ("rows", "cols", "sub")
    layout = Layout(activations.shape[1] // BLK)
    team, teams, held = layout.team, layout.teams, layout.held
    subs, columns, token_group = layout.subs, layout.columns, layout.token_group

    def exchange(pieces):
        arrived = [pieces[0]]
        for shift, piece in zip(layout.shifts[1:], pieces[1:]):
            route = [(t, t ^ shift) for t in range(token_group)]
            arrived.append(lax.ppermute(piece, token_axes, route))
        return arrived

    def shared(terms):
        gathered = [terms]
        for step in range(1, teams):
            route = [(t, (t + step * team) % token_group) for t in range(token_group)]
            gathered.append(lax.ppermute(terms, token_axes, route))
        return gathered

    def along(block, distance):
        route = []
        for at in range(columns * team):
            if 0 <= at + distance < columns * team:
                for group in range(teams):
                    ends = []
                    for one in (at, at + distance):
                        home, inner = divmod(one, team)
                        inner = team - 1 - inner if home % 2 else inner
                        row, sub = divmod(group * team + inner, subs)
                        ends.append((row * columns + home) * subs + sub)
                    route.append(tuple(ends))
        return lax.ppermute(block, all_axes, route)

    def always():
        return lax.axis_index("cols") >= 0

    pieces = pack(layout, plan, activations)
    pieces = [pieces[g * team : (g + 1) * team] for g in range(held)]
    arrived = []
    for piece in pieces:
        if arrived:
            piece, arrived[-1] = lax.optimization_barrier((piece, arrived[-1]))
        arrived.append(exchange(piece))
    ready = [gather_terms(layout, piece) for piece in arrived]
    summed = [shared(terms) for _, terms in ready]

    top = held - 1

    def next_terms(g, uppers, lowers, edge, leaving, arriving):
        if g == 0:
            from_above, pick_upper = ([uppers[0]], [arriving]), layout.first
        elif g == 1:
            from_above, pick_upper = ([lowers[0]], [uppers[0]]), layout.first
        else:
            from_above, pick_upper = ([uppers[g - 1]],) * 2, always
        if g == top:
            from_below, pick_lower = (edge, [leaving]), layout.final
        else:
            from_below, pick_lower = ([lowers[g + 1]],) * 2, always
        blocks, terms = choose_terms((pick_upper, pick_lower), from_above, from_below)
        return blocks, shared(terms)

    for g in range(1, held):
        summed[0][0], summed[g][0] = lax.optimization_barrier((summed[0][0], summed[g][0]))
    uppers, lowers, nexts = [None] * held, [None] * held, [None] * held
    leaving = None
    for g in range(top):
        factors = factor(summed[g])
        lowers[g] = turn(1, ready[g][0], factors)
        if g == 0:
            leaving = along(lowers[0], -1)
        uppers[g] = turn(0, ready[g][0], factors)
    factors = factor(summed[top])
    if top:
        nexts[top] = next_terms(top, uppers, lowers, [ready[top][0], factors], leaving, None)
        factors, nexts[top][1][0] = lax.optimization_barrier((factors, nexts[top][1][0]))
    uppers[top] = turn(0, ready[top][0], factors)
    if top:
        arriving = along(uppers[top], 1)
        lowers[top] = turn(1, ready[top][0], factors)
    else:
        lowers[0] = turn(1, ready[0][0], factors)
        arriving = along(jnp.where(layout.first(), lowers[0], uppers[0]), 1)
        leaving = along(lowers[0], -1)
    for g in reversed(range(held)):
        if nexts[g] is None:
            nexts[g] = next_terms(g, uppers, lowers, [uppers[top]], leaving, arriving)

    for g in range(1, held):
        nexts[0][1][0], nexts[g][1][0] = lax.optimization_barrier((nexts[0][1][0], nexts[g][1][0]))
    far = [i for i, shift in enumerate(layout.shifts) if shift >= subs]
    near = [i for i, shift in enumerate(layout.shifts) if shift < subs]
    results = [None] * held
    for g in reversed(range(held)):
        blocks, terms = nexts[g]
        factors = factor(terms)
        sent = [None] * team
        for partners in (far, near):
            if partners:
                for i, piece in zip(partners, turn_out(layout, partners, blocks, factors)):
                    sent[i] = piece
        results[g] = exchange(sent)
    return unpack(layout, [piece for result in results for piece in result])


def solution(mesh):
    in_specs = (P(("groups", "rows", "sub"), "cols"), P())
    out_specs = P(("groups", "rows", "sub"), "cols")
    return jax.shard_map(
        on_device, mesh=mesh, in_specs=in_specs, out_specs=out_specs, check_vma=False
    )
```

```python
import functools

import jax
import jax.numpy as jnp
from jax import lax
from jax.experimental import pallas as pl
from jax.experimental.pallas import tpu as pltpu
from jax.sharding import PartitionSpec as P

BLK = 256
ROUNDS = 2
PANEL = 64
HALF = 2 * PANEL
SUBLANES = 8

epsilon = 1e-06
HIGH = lax.Precision.HIGHEST
VMEM_LIMIT = 16 * 1024 * 1024
PACK_VMEM_LIMIT = 61 * 1024 * 1024
TEAM_CHIPS = 2
SQUARES = 8
UP_PARTS = 2
CHUNK = 256


def contract(a, b, a_dim, b_dim):
    return lax.dot_general(
        a, b, (((a_dim,), (b_dim,)), ((), ())), precision=HIGH, preferred_element_type=jnp.float32
    )


def iota2(shape, dim):
    return lax.broadcasted_iota(jnp.int32, shape, dim)


def reciprocal(x):
    guess = pl.reciprocal(x, approx=True)
    return guess, 2.0 - x * guess


def eliminate(blocks):
    width = 2 * PANEL
    shape = (SUBLANES, width)
    tiles = PANEL // SUBLANES
    lines = range(SUBLANES)
    ident = jnp.where(
        iota2((PANEL, width), 0) == lax.rem(iota2((PANEL, width), 1), PANEL), 1.0, 0.0
    ).astype(jnp.float32)
    sub = iota2(shape, 0)
    halves = jnp.where(iota2(shape, 1) < PANEL, 0, PANEL)
    whole = jnp.concatenate(blocks, axis=1)
    parts = [whole[SUBLANES * v : SUBLANES * (v + 1)] for v in range(tiles)]
    sides = [ident[SUBLANES * v : SUBLANES * (v + 1)] for v in range(tiles)]
    outs = []

    def spread(tile, line):
        return jnp.broadcast_to(tile[line : line + 1, :], shape)

    for q in range(tiles):
        columns = [
            [
                jnp.take_along_axis(parts[v], halves + (SUBLANES * q + j), axis=1)
                for j in lines
            ]
            for v in range(q, tiles)
        ]
        entry = [[spread(columns[0][j], i) for j in range(i + 1)] for i in lines]
        rows = [spread(parts[q], i) for i in lines]
        side_rows = [spread(sides[q], i) for i in lines]
        inverses = []
        for s in lines:
            guess, mend = reciprocal(entry[s][s])
            inverses.append(guess * mend)
            factors = {i: (entry[i][s] * guess) * mend for i in range(s + 1, SUBLANES)}
            for i in range(s + 1, SUBLANES):
                for j in range(s + 1, i + 1):
                    entry[i][j] = entry[i][j] - factors[i] * entry[j][s]
            for i in range(s + 1, SUBLANES):
                rows[i] = rows[i] - factors[i] * rows[s]
                side_rows[i] = side_rows[i] - factors[i] * side_rows[s]
        for v in range(q + 1, tiles):
            factors = []
            for s in lines:
                value = columns[v - q][s]
                for t in range(s):
                    value = value - factors[t] * entry[s][t]
                factors.append(value * inverses[s])
            for s in lines:
                parts[v] = parts[v] - factors[s] * rows[s]
                sides[v] = sides[v] - factors[s] * side_rows[s]
        tile = side_rows[0] * lax.rsqrt(entry[0][0])
        for i in lines[1:]:
            tile = jnp.where(sub == i, side_rows[i] * lax.rsqrt(entry[i][i]), tile)
        outs.append(tile)
    out = jnp.concatenate(outs, axis=0)
    return out[:, :PANEL], out[:, PANEL:]


def inverse_factors(work_ref):
    lane = iota2((PANEL, BLK), 1)
    line = iota2((PANEL, BLK), 0)
    first_ident = jnp.where(line == lane, 1.0, 0.0).astype(jnp.float32)
    second_ident = jnp.where(line == lane - PANEL, 1.0, 0.0).astype(jnp.float32)
    first_own = lane < PANEL
    own = lane < HALF
    second_own = jnp.logical_and(own, lane >= PANEL)
    lane_below = iota2((HALF, BLK), 1)
    first_own_below = lane_below < PANEL
    own_below = lane_below < HALF

    def step(h, _):
        waiting = jnp.full((PANEL, BLK), h, jnp.int32) == 0
        over = jnp.logical_not(waiting)
        panels = [jnp.concatenate([work_ref[m, h, h], work_ref[m, h, 1 - h]], axis=1) for m in range(2)]
        belows = [
            jnp.concatenate([work_ref[m, 1 - h, h], work_ref[m, 1 - h, 1 - h]], axis=1)
            for m in range(2)
        ]
        invs = eliminate([panel[:PANEL, :PANEL] for panel in panels])
        tops, seconds = [], []
        for m in range(2):
            rows = contract(invs[m], jnp.where(first_own, first_ident, panels[m][:PANEL]), 1, 0)
            factors = jnp.where(jnp.logical_or(own, waiting), rows, 0.0)
            change = contract(factors[:, PANEL:], rows, 0, 0)
            seconds.append(jnp.where(first_own, 0.0, panels[m][PANEL:]) - change[:PANEL])
            belows[m] = jnp.where(first_own_below, 0.0, belows[m]) - change[PANEL:]
            keep = jnp.logical_or(first_own, jnp.logical_and(jnp.logical_not(own), over))
            tops.append(jnp.where(keep, rows, 0.0))
        invs = eliminate([second[:, PANEL:HALF] for second in seconds])
        for m in range(2):
            rows = contract(invs[m], jnp.where(second_own, second_ident, seconds[m]), 1, 0)
            factors = jnp.where(waiting, rows, 0.0)
            change = contract(factors[:, HALF:], rows, 0, 0)
            below = jnp.where(own_below, jnp.where(first_own_below, belows[m], 0.0), belows[m]) - change
            done = jnp.concatenate([tops[m], jnp.where(jnp.logical_or(own, over), rows, 0.0)], axis=0)
            work_ref[m, h, h] = done[:, :HALF]
            work_ref[m, h, 1 - h] = done[:, HALF:]
            work_ref[m, 1 - h, h] = below[:, :HALF]
            work_ref[m, 1 - h, 1 - h] = below[:, HALF:]
        return 0

    lax.fori_loop(0, 2, step, 0)


def pair_terms(blocks_ref, terms_ref):
    tokens = blocks_ref.shape[1]
    chunk = min(CHUNK, tokens)
    line = iota2((SQUARES, BLK), 0)
    terms_ref[...] = jnp.zeros_like(terms_ref)

    def step(i, _):
        at = pl.ds(pl.multiple_of(i * chunk, chunk), chunk)
        upper, lower = blocks_ref[0, at, :], blocks_ref[1, at, :]
        upper_sq = jnp.sum(upper * upper, axis=0, keepdims=True)
        lower_sq = jnp.sum(lower * lower, axis=0, keepdims=True)
        squares = jnp.where(line == 0, upper_sq, jnp.where(line == 1, lower_sq, 0.0))
        terms_ref[:BLK] += contract(upper, lower, 0, 0)
        terms_ref[BLK:] += squares
        return 0

    lax.fori_loop(0, tokens // chunk, step, 0)


SMEM_SPEC = pl.BlockSpec(memory_space=pltpu.SMEM)
VMEM_SPEC = pl.BlockSpec(memory_space=pltpu.VMEM)
HBM_SPEC = pl.BlockSpec(memory_space=pltpu.HBM)


def call(kernel, name, out_shape, in_specs, out_specs, scratch, micros, vmem=VMEM_LIMIT):
    return pl.pallas_call(
        kernel,
        out_shape=out_shape,
        in_specs=in_specs,
        out_specs=out_specs,
        scratch_shapes=scratch,
        compiler_params=pltpu.CompilerParams(vmem_limit_bytes=vmem),
        cost_estimate=pl.CostEstimate(
            flops=int(micros * 1e9), bytes_accessed=1 << 20, transcendentals=0
        ),
        name=name,
    )


def f32(*shape):
    return jax.ShapeDtypeStruct(shape, jnp.float32)


class Layout:
    def __init__(self, block_count):
        self.block_count = block_count
        self.pairs = block_count // 2
        self.subs = lax.axis_size("sub")
        self.columns = lax.axis_size("cols")
        self.token_group = lax.axis_size("rows") * self.subs
        self.team = min(self.pairs, TEAM_CHIPS * self.subs, self.token_group)
        self.teams = self.token_group // self.team
        self.held = self.pairs // self.team
        assert self.team * self.teams == self.token_group
        assert self.team * self.held == self.pairs and self.team & (self.team - 1) == 0
        self.shifts = [0] + list(range(self.team - 1, 0, -1))

    def member(self):
        return lax.rem(lax.axis_index("rows") * self.subs + lax.axis_index("sub"), self.team)

    def partner(self, i):
        return lax.bitwise_xor(self.member(), jnp.int32(self.shifts[i]))

    def place_of(self, member):
        backwards = lax.rem(lax.axis_index("cols"), 2) == 1
        return jnp.where(backwards, self.team - 1 - member, member)

    def pair_at(self, g, i):
        return self.place_of(self.partner(i)) * self.held + g

    def first(self):
        return jnp.logical_and(lax.axis_index("cols") == 0, self.place_of(self.member()) == 0)

    def final(self):
        return jnp.logical_and(
            lax.axis_index("cols") == self.columns - 1,
            self.place_of(self.member()) == self.team - 1,
        )


def pack_kernel(layout, items, plan_ref, x_ref, *refs):
    outs, in_sem = refs[:-1], refs[-1]
    base = lax.axis_index("cols") * layout.block_count
    loads = []
    for i, (item, out) in enumerate(zip(items, outs)):
        pair = layout.pair_at(*item)
        for half in range(2):
            block = plan_ref[0, base + 2 * pair + half] - base
            start = pl.multiple_of(block * BLK, BLK)
            loads.append(
                pltpu.make_async_copy(
                    x_ref.at[:, pl.ds(start, BLK)],
                    out.at[:, half * BLK : (half + 1) * BLK],
                    in_sem.at[2 * i + half],
                )
            )
    for load in loads:
        load.start()
    for load in loads:
        load.wait()


def pack(layout, items, plan, x, vmem):
    count = len(items)
    return call(
        functools.partial(pack_kernel, layout, items),
        "pack",
        [f32(x.shape[0], 2 * BLK)] * count,
        [SMEM_SPEC, HBM_SPEC],
        [VMEM_SPEC] * count,
        [pltpu.SemaphoreType.DMA((2 * count,))],
        2,
        vmem,
    )(plan, x)


def unpack_kernel(layout, *refs):
    pieces, out_ref, held, in_sem, out_sem = refs[:-4], *refs[-4:]
    width = 2 * BLK
    loads, stores = [], []
    for i, piece in enumerate(pieces):
        start = pl.multiple_of(layout.pair_at(*divmod(i, layout.team)) * width, width)
        loads.append(pltpu.make_async_copy(piece, held.at[i], in_sem.at[i]))
        stores.append(
            pltpu.make_async_copy(held.at[i], out_ref.at[:, pl.ds(start, width)], out_sem.at[i])
        )
    for load in loads:
        load.start()
    for load, store in zip(loads, stores):
        load.wait()
        store.start()
    for store in stores:
        store.wait()


def unpack(layout, pieces):
    rows, width = pieces[0].shape
    count = len(pieces)
    return call(
        functools.partial(unpack_kernel, layout),
        "unpack",
        f32(rows, count * width),
        [HBM_SPEC] * count,
        HBM_SPEC,
        [
            pltpu.VMEM((count, rows, width), jnp.float32),
            pltpu.SemaphoreType.DMA((count,)),
            pltpu.SemaphoreType.DMA((count,)),
        ],
        3,
    )(*pieces)


def gather_terms_kernel(layout, *refs):
    pieces, (blocks_ref, terms_ref) = refs[:-2], refs[-2:]
    rows = pieces[0].shape[0]
    for i, piece in enumerate(pieces):
        at = pl.ds(pl.multiple_of(layout.partner(i) * rows, rows), rows)
        blocks_ref[0, at, :] = piece[:, :BLK]
        blocks_ref[1, at, :] = piece[:, BLK:]
    pair_terms(blocks_ref, terms_ref)


def gather_terms(layout, pieces):
    tokens = pieces[0].shape[0] * len(pieces)
    return call(
        functools.partial(gather_terms_kernel, layout),
        "gather_terms",
        [f32(2, tokens, BLK), f32(BLK + SQUARES, BLK)],
        [VMEM_SPEC] * len(pieces),
        [VMEM_SPEC] * 2,
        [],
        2,
    )(*pieces)


def choose_terms_kernel(pick_upper, pick_lower, uppers, lowers, *refs):
    inputs, (blocks_ref, terms_ref) = refs[:-2], refs[-2:]

    def fetch(m, at):
        refs = [inputs[i] for i in at]
        if len(refs[0].shape) == 3:
            pair_ref, inv_ref = refs
            chunk = min(CHUNK, pair_ref.shape[1])

            def step(i, _):
                rows = pl.ds(pl.multiple_of(i * chunk, chunk), chunk)
                blocks_ref[m, rows, :] = turned(pair_ref[0, rows, :], pair_ref[1, rows, :], inv_ref, 0)
                return 0

            lax.fori_loop(0, pair_ref.shape[1] // chunk, step, 0)
        else:
            rows = refs[0].shape[0]
            for i, ref in enumerate(refs):
                blocks_ref[m, i * rows : (i + 1) * rows, :] = ref[...]

    for m, (pick, choices) in enumerate(((pick_upper, uppers), (pick_lower, lowers))):
        chosen = pick()
        pl.when(chosen)(functools.partial(fetch, m, choices[0]))
        pl.when(jnp.logical_not(chosen))(functools.partial(fetch, m, choices[1]))
    pair_terms(blocks_ref, terms_ref)


def choose_terms(picks, uppers, lowers):
    tokens = sum(part.shape[0] for part in uppers[0])
    inputs, places = [], []
    for choice in (*uppers, *lowers):
        places.append(tuple(range(len(inputs), len(inputs) + len(choice))))
        inputs.extend(choice)
    return call(
        functools.partial(choose_terms_kernel, *picks, places[:2], places[2:]),
        "choose_terms",
        [f32(2, tokens, BLK), f32(BLK + SQUARES, BLK)],
        [VMEM_SPEC] * len(inputs),
        [VMEM_SPEC] * 2,
        [],
        2,
    )(*inputs)


def total_terms(refs):
    total = refs[0][...]
    for ref in refs[1:]:
        total = total + ref[...]
    return total


def factor_kernel(*refs):
    terms, (inv_ref, corr_ref, work_ref) = refs[:-3], refs[-3:]
    terms = total_terms(terms)
    square = (BLK, BLK)
    diagonal = iota2(square, 0) == iota2(square, 1)
    upper_sq, lower_sq = terms[BLK : BLK + 1], terms[BLK + 1 : BLK + 2]
    upper_sq = jnp.sum(
        jnp.where(diagonal, jnp.broadcast_to(upper_sq, square), 0.0), axis=1, keepdims=True
    )
    corr = terms[:BLK] * lax.rsqrt(upper_sq + epsilon) * lax.rsqrt(lower_sq + epsilon)
    corr_ref[0] = corr
    corr_ref[1] = -jnp.transpose(corr)

    def gram(m, _):
        corr = corr_ref[m]
        whole = jnp.where(diagonal, 1.0, 0.0).astype(jnp.float32) + contract(corr, corr, 1, 1)
        for r in range(2):
            for c in range(2):
                work_ref[m, r, c] = whole[HALF * r : HALF * (r + 1), HALF * c : HALF * (c + 1)]
        return 0

    def widen(m, _):
        whole = jnp.concatenate(
            [jnp.concatenate([work_ref[m, r, 0], work_ref[m, r, 1]], axis=1) for r in range(2)],
            axis=0,
        )
        inv_ref[m, :, :BLK] = whole
        inv_ref[m, :, BLK:] = contract(whole, corr_ref[m], 1, 0)
        return 0

    lax.fori_loop(0, 2, gram, 0)
    inverse_factors(work_ref)
    lax.fori_loop(0, 2, widen, 0)


def factor(terms):
    return call(
        factor_kernel,
        "factor",
        f32(2, BLK, 2 * BLK),
        [VMEM_SPEC] * len(terms),
        VMEM_SPEC,
        [
            pltpu.VMEM((2, BLK, BLK), jnp.float32),
            pltpu.VMEM((2, 2, 2, HALF, HALF), jnp.float32),
        ],
        11,
    )(*terms)


def turned(own, other, inv_ref, m):
    return contract(own, inv_ref[m, :, :BLK], 1, 1) + contract(other, inv_ref[m, :, BLK:], 1, 1)


def turn_kernel(m, blocks_ref, inv_ref, *out_refs):
    chunk = min(CHUNK, out_refs[0].shape[0])
    for part, out_ref in enumerate(out_refs):
        first = part * out_ref.shape[0]

        def step(i, _):
            start = pl.multiple_of(i * chunk, chunk)
            at = pl.ds(first + start, chunk)
            out_ref[pl.ds(start, chunk), :] = turned(
                blocks_ref[m, at, :], blocks_ref[1 - m, at, :], inv_ref, m
            )
            return 0

        lax.fori_loop(0, out_ref.shape[0] // chunk, step, 0)


def turn(m, blocks, factors, parts=1):
    out = call(
        functools.partial(turn_kernel, m),
        "turn",
        [f32(blocks.shape[1] // parts, BLK)] * parts,
        [VMEM_SPEC] * 2,
        [VMEM_SPEC] * parts,
        [],
        2,
    )(blocks, factors)
    return list(out)


def turn_out_kernel(layout, partners, blocks_ref, inv_ref, *refs):
    outs, out_ref = refs[:-1], refs[-1]
    rows = outs[0].shape[0]
    spans = [pl.ds(pl.multiple_of(layout.partner(i) * rows, rows), rows) for i in partners]

    def step(m, _):
        own = jnp.concatenate([blocks_ref[m, at, :] for at in spans], axis=0)
        other = jnp.concatenate([blocks_ref[1 - m, at, :] for at in spans], axis=0)
        out_ref[m] = turned(own, other, inv_ref, m)
        return 0

    lax.fori_loop(0, 2, step, 0)
    for i, out in enumerate(outs):
        out[:, :BLK] = out_ref[0, i * rows : (i + 1) * rows, :]
        out[:, BLK:] = out_ref[1, i * rows : (i + 1) * rows, :]


def turn_out(layout, partners, blocks, factors):
    rows = blocks.shape[1] // layout.team
    count = len(partners)
    return call(
        functools.partial(turn_out_kernel, layout, partners),
        "turn_out",
        [f32(rows, 2 * BLK)] * count,
        [VMEM_SPEC] * 2,
        [VMEM_SPEC] * count,
        [pltpu.VMEM((2, rows * count, BLK), jnp.float32)],
        2,
    )(blocks, factors)


def on_device(activations, plan):
    token_axes = ("rows", "sub")
    all_axes = ("rows", "cols", "sub")
    layout = Layout(activations.shape[1] // BLK)
    team, teams, held = layout.team, layout.teams, layout.held
    subs, columns, token_group = layout.subs, layout.columns, layout.token_group

    def exchange(pieces):
        arrived = [pieces[0]]
        for shift, piece in zip(layout.shifts[1:], pieces[1:]):
            route = [(t, t ^ shift) for t in range(token_group)]
            arrived.append(lax.ppermute(piece, token_axes, route))
        return arrived

    def shared(terms):
        gathered = [terms]
        for step in range(1, teams):
            route = [(t, (t + step * team) % token_group) for t in range(token_group)]
            gathered.append(lax.ppermute(terms, token_axes, route))
        return gathered

    def along(block, distance):
        route = []
        for at in range(columns * team):
            if 0 <= at + distance < columns * team:
                for group in range(teams):
                    ends = []
                    for one in (at, at + distance):
                        home, inner = divmod(one, team)
                        inner = team - 1 - inner if home % 2 else inner
                        row, sub = divmod(group * team + inner, subs)
                        ends.append((row * columns + home) * subs + sub)
                    route.append(tuple(ends))
        return lax.ppermute(block, all_axes, route)

    def always():
        return lax.axis_index("cols") >= 0

    early = [(0, i) for i in range(1, team)]
    late = [(0, 0)] + [(g, i) for g in range(1, held) for i in range(team)]
    packed = list(pack(layout, early, plan, activations, PACK_VMEM_LIMIT))
    plan, packed[0] = lax.optimization_barrier((plan, packed[0]))
    pieces = dict(zip(early, packed))
    pieces.update(zip(late, pack(layout, late, plan, activations, VMEM_LIMIT)))
    arrived = []
    for g in range(held):
        piece = [pieces[g, i] for i in range(team)]
        if arrived:
            piece, arrived[-1] = lax.optimization_barrier((piece, arrived[-1]))
        arrived.append(exchange(piece))
    ready = [gather_terms(layout, piece) for piece in arrived]
    summed = [shared(terms) for _, terms in ready]
    top = held - 1

    def next_terms(g, uppers, lowers, edge, leaving, arriving):
        if g == 0:
            from_above, pick_upper = (uppers[0], arriving), layout.first
        elif g == 1:
            from_above, pick_upper = (lowers[0], uppers[0]), layout.first
        else:
            from_above, pick_upper = (uppers[g - 1],) * 2, always
        if g == top:
            from_below, pick_lower = (edge, leaving), layout.final
        else:
            from_below, pick_lower = (lowers[g + 1],) * 2, always
        blocks, terms = choose_terms((pick_upper, pick_lower), from_above, from_below)
        return blocks, shared(terms)

    for g in range(1, held):
        summed[0][0], summed[g][0] = lax.optimization_barrier((summed[0][0], summed[g][0]))
    uppers, lowers, nexts = [None] * held, [None] * held, [None] * held
    leaving = None
    for g in range(top):
        factors = factor(summed[g])
        lowers[g] = turn(1, ready[g][0], factors)
        if g == 0:
            leaving = [along(part, -1) for part in lowers[0]]
        uppers[g] = turn(0, ready[g][0], factors)
    factors = factor(summed[top])
    if top:
        nexts[top] = next_terms(top, uppers, lowers, [ready[top][0], factors], leaving, None)
        factors, nexts[top][1][0] = lax.optimization_barrier((factors, nexts[top][1][0]))
    uppers[top] = turn(0, ready[top][0], factors, UP_PARTS)
    if top:
        arriving = [along(part, 1) for part in uppers[top]]
        lowers[top] = turn(1, ready[top][0], factors)
        for term in nexts[top][1]:
            lowers[top][0], term = lax.optimization_barrier((lowers[top][0], term))
    else:
        lowers[0] = turn(1, ready[0][0], factors, UP_PARTS)
        arriving = [
            along(jnp.where(layout.first(), low, up), 1) for low, up in zip(lowers[0], uppers[0])
        ]
        leaving = [along(part, -1) for part in lowers[0]]
    for g in reversed(range(held)):
        if nexts[g] is None:
            nexts[g] = next_terms(g, uppers, lowers, uppers[top], leaving, arriving)

    for g in range(1, held):
        nexts[0][1][0], nexts[g][1][0] = lax.optimization_barrier((nexts[0][1][0], nexts[g][1][0]))
    far = [i for i, shift in enumerate(layout.shifts) if shift >= subs]
    near = [i for i, shift in enumerate(layout.shifts) if shift < subs]
    results = [None] * held
    for g in reversed(range(held)):
        blocks, terms = nexts[g]
        factors = factor(terms)
        sent = [None] * team
        for partners in (far, near):
            if partners:
                for i, piece in zip(partners, turn_out(layout, partners, blocks, factors)):
                    sent[i] = piece
        results[g] = exchange(sent)
    return unpack(layout, [piece for result in results for piece in result])


def solution(mesh):
    in_specs = (P(("groups", "rows", "sub"), "cols"), P())
    out_specs = P(("groups", "rows", "sub"), "cols")
    return jax.shard_map(
        on_device, mesh=mesh, in_specs=in_specs, out_specs=out_specs, check_vma=False
    )
```

```python
import functools

import jax
import jax.numpy as jnp
from jax import lax
from jax.experimental import pallas as pl
from jax.experimental.pallas import tpu as pltpu
from jax.sharding import PartitionSpec as P

BLK = 256
ROUNDS = 2
PANEL = 64
HALF = 2 * PANEL
SUBLANES = 8

epsilon = 1e-06
HIGH = lax.Precision.HIGHEST
VMEM_LIMIT = 16 * 1024 * 1024
PACK_VMEM_LIMIT = 61 * 1024 * 1024
TEAM_CHIPS = 2
SQUARES = 8
UP_PARTS = 2
CHUNK = 256


def contract(a, b, a_dim, b_dim):
    return lax.dot_general(
        a, b, (((a_dim,), (b_dim,)), ((), ())), precision=HIGH, preferred_element_type=jnp.float32
    )


def iota2(shape, dim):
    return lax.broadcasted_iota(jnp.int32, shape, dim)


def reciprocal(x):
    guess = pl.reciprocal(x, approx=True)
    return guess, 2.0 - x * guess


def split(x):
    high = x.astype(jnp.bfloat16).astype(jnp.float32)
    rest = x - high
    middle = rest.astype(jnp.bfloat16).astype(jnp.float32)
    return high, middle, rest - middle


def packed_product(doubled, rows):
    high, middle, low = split(doubled)
    mixed = jnp.where(iota2(doubled.shape, 1) < PANEL, high, low)
    left = jnp.concatenate([part.astype(jnp.bfloat16) for part in (high, middle, mixed)], axis=1)
    high, middle, low = (part.astype(jnp.bfloat16) for part in split(rows))
    right = jnp.concatenate([high, middle, high, middle, low, high], axis=0)
    return lax.dot_general(
        left, right, (((1,), (0,)), ((), ())), preferred_element_type=jnp.float32
    )


def doubled_transpose(x):
    return jnp.transpose(jnp.concatenate([x, x], axis=0))


def eliminate(blocks):
    width = 2 * PANEL
    shape = (SUBLANES, width)
    tiles = PANEL // SUBLANES
    lines = range(SUBLANES)
    ident = jnp.where(
        iota2((PANEL, width), 0) == lax.rem(iota2((PANEL, width), 1), PANEL), 1.0, 0.0
    ).astype(jnp.float32)
    sub = iota2(shape, 0)
    halves = jnp.where(iota2(shape, 1) < PANEL, 0, PANEL)
    whole = jnp.concatenate(blocks, axis=1)
    parts = [whole[SUBLANES * v : SUBLANES * (v + 1)] for v in range(tiles)]
    sides = [ident[SUBLANES * v : SUBLANES * (v + 1)] for v in range(tiles)]
    outs = []

    def spread(tile, line):
        return jnp.broadcast_to(tile[line : line + 1, :], shape)

    for q in range(tiles):
        columns = [
            [
                jnp.take_along_axis(parts[v], halves + (SUBLANES * q + j), axis=1)
                for j in lines
            ]
            for v in range(q, tiles)
        ]
        entry = [[spread(columns[0][j], i) for j in range(i + 1)] for i in lines]
        rows = [spread(parts[q], i) for i in lines]
        side_rows = [spread(sides[q], i) for i in lines]
        inverses = []
        for s in lines:
            guess, mend = reciprocal(entry[s][s])
            inverses.append(guess * mend)
            factors = {i: (entry[i][s] * guess) * mend for i in range(s + 1, SUBLANES)}
            for i in range(s + 1, SUBLANES):
                for j in range(s + 1, i + 1):
                    entry[i][j] = entry[i][j] - factors[i] * entry[j][s]
            for i in range(s + 1, SUBLANES):
                rows[i] = rows[i] - factors[i] * rows[s]
                side_rows[i] = side_rows[i] - factors[i] * side_rows[s]
        for v in range(q + 1, tiles):
            factors = []
            for s in lines:
                value = columns[v - q][s]
                for t in range(s):
                    value = value - factors[t] * entry[s][t]
                factors.append(value * inverses[s])
            for s in lines:
                parts[v] = parts[v] - factors[s] * rows[s]
                sides[v] = sides[v] - factors[s] * side_rows[s]
        tile = side_rows[0] * lax.rsqrt(entry[0][0])
        for i in lines[1:]:
            tile = jnp.where(sub == i, side_rows[i] * lax.rsqrt(entry[i][i]), tile)
        outs.append(tile)
    out = jnp.concatenate(outs, axis=0)
    turned_out = pltpu.roll(out, PANEL, 1)
    left = iota2(out.shape, 1) < PANEL
    return jnp.where(left, out, turned_out), jnp.where(left, turned_out, out)


def half_step(work_ref, h):
    lane = iota2((PANEL, BLK), 1)
    line = iota2((PANEL, BLK), 0)
    first_ident = jnp.where(line == lane, 1.0, 0.0).astype(jnp.float32)
    second_ident = jnp.where(line == lane - PANEL, 1.0, 0.0).astype(jnp.float32)
    first_own = lane < PANEL
    own = lane < HALF
    second_own = jnp.logical_and(own, lane >= PANEL)
    lane_below = iota2((HALF, BLK), 1)
    other = 1 - h
    known = isinstance(h, int)
    others_rows = not known or h == 0
    over = jnp.full((PANEL, BLK), h, jnp.int32) == 1

    def for_others(rows):
        return rows if known else jnp.where(jnp.logical_or(own, jnp.logical_not(over)), rows, 0.0)

    panels = [jnp.concatenate([work_ref[m, h, h], work_ref[m, h, other]], axis=1) for m in range(2)]
    invs = eliminate([panel[:PANEL, :PANEL] for panel in panels])
    tops, seconds, belows = [], [], []
    for m in range(2):
        rows = packed_product(invs[m], jnp.where(first_own, first_ident, panels[m][:PANEL]))
        factors = for_others(rows) if others_rows else rows[:, :HALF]
        change = packed_product(doubled_transpose(factors)[PANEL:], rows)
        seconds.append(jnp.where(first_own, 0.0, panels[m][PANEL:]) - change[:PANEL])
        if others_rows:
            below = jnp.concatenate([work_ref[m, other, h], work_ref[m, other, other]], axis=1)
            belows.append(jnp.where(lane_below < PANEL, 0.0, below) - change[PANEL:])
        keep = jnp.logical_or(first_own, jnp.logical_and(over, jnp.logical_not(own)))
        tops.append(jnp.where(keep, rows, 0.0))
    invs = eliminate([second[:, PANEL:HALF] for second in seconds])
    for m in range(2):
        rows = packed_product(invs[m], jnp.where(second_own, second_ident, seconds[m]))
        if others_rows:
            factors = for_others(rows)[:, HALF:]
            change = packed_product(doubled_transpose(factors), rows)
            gone = jnp.logical_and(lane_below >= PANEL, lane_below < HALF)
            below = jnp.where(gone, 0.0, belows[m]) - change
            work_ref[m, other, h] = below[:, :HALF]
            work_ref[m, other, other] = below[:, HALF:]
        rows = jnp.where(jnp.logical_or(own, over), rows, 0.0)
        done = jnp.concatenate([tops[m], rows], axis=0)
        work_ref[m, h, h] = done[:, :HALF]
        work_ref[m, h, other] = done[:, HALF:]


def pair_terms(blocks_ref, terms_ref):
    tokens = blocks_ref.shape[1]
    chunk = min(CHUNK, tokens)
    line = iota2((SQUARES, BLK), 0)
    terms_ref[...] = jnp.zeros_like(terms_ref)

    def step(i, _):
        at = pl.ds(pl.multiple_of(i * chunk, chunk), chunk)
        upper, lower = blocks_ref[0, at, :], blocks_ref[1, at, :]
        upper_sq = jnp.sum(upper * upper, axis=0, keepdims=True)
        lower_sq = jnp.sum(lower * lower, axis=0, keepdims=True)
        squares = jnp.where(line == 0, upper_sq, jnp.where(line == 1, lower_sq, 0.0))
        terms_ref[:BLK] += contract(upper, lower, 0, 0)
        terms_ref[BLK:] += squares
        return 0

    lax.fori_loop(0, tokens // chunk, step, 0)


SMEM_SPEC = pl.BlockSpec(memory_space=pltpu.SMEM)
VMEM_SPEC = pl.BlockSpec(memory_space=pltpu.VMEM)
HBM_SPEC = pl.BlockSpec(memory_space=pltpu.HBM)


def call(kernel, name, out_shape, in_specs, out_specs, scratch, micros, vmem=VMEM_LIMIT):
    return pl.pallas_call(
        kernel,
        out_shape=out_shape,
        in_specs=in_specs,
        out_specs=out_specs,
        scratch_shapes=scratch,
        compiler_params=pltpu.CompilerParams(vmem_limit_bytes=vmem),
        cost_estimate=pl.CostEstimate(
            flops=int(micros * 1e9), bytes_accessed=1 << 20, transcendentals=0
        ),
        name=name,
    )


def f32(*shape):
    return jax.ShapeDtypeStruct(shape, jnp.float32)


class Layout:
    def __init__(self, block_count):
        self.block_count = block_count
        self.pairs = block_count // 2
        self.subs = lax.axis_size("sub")
        self.columns = lax.axis_size("cols")
        self.token_group = lax.axis_size("rows") * self.subs
        self.team = min(self.pairs, TEAM_CHIPS * self.subs, self.token_group)
        self.teams = self.token_group // self.team
        self.held = self.pairs // self.team
        assert self.team * self.teams == self.token_group
        assert self.team * self.held == self.pairs and self.team & (self.team - 1) == 0
        self.shifts = [0] + list(range(self.team - 1, 0, -1))

    def member(self):
        return lax.rem(lax.axis_index("rows") * self.subs + lax.axis_index("sub"), self.team)

    def partner(self, i):
        return lax.bitwise_xor(self.member(), jnp.int32(self.shifts[i]))

    def place_of(self, member):
        backwards = lax.rem(lax.axis_index("cols"), 2) == 1
        return jnp.where(backwards, self.team - 1 - member, member)

    def pair_at(self, g, i):
        return self.place_of(self.partner(i)) * self.held + g

    def first(self):
        return jnp.logical_and(lax.axis_index("cols") == 0, self.place_of(self.member()) == 0)

    def final(self):
        return jnp.logical_and(
            lax.axis_index("cols") == self.columns - 1,
            self.place_of(self.member()) == self.team - 1,
        )


def pack_kernel(layout, items, plan_ref, x_ref, *refs):
    outs, in_sem = refs[:-1], refs[-1]
    base = lax.axis_index("cols") * layout.block_count
    loads = []
    for i, (item, out) in enumerate(zip(items, outs)):
        pair = layout.pair_at(*item)
        for half in range(2):
            block = plan_ref[0, base + 2 * pair + half] - base
            start = pl.multiple_of(block * BLK, BLK)
            loads.append(
                pltpu.make_async_copy(
                    x_ref.at[:, pl.ds(start, BLK)],
                    out.at[:, half * BLK : (half + 1) * BLK],
                    in_sem.at[2 * i + half],
                )
            )
    for load in loads:
        load.start()
    for load in loads:
        load.wait()


def pack(layout, items, plan, x, vmem):
    count = len(items)
    return call(
        functools.partial(pack_kernel, layout, items),
        "pack",
        [f32(x.shape[0], 2 * BLK)] * count,
        [SMEM_SPEC, HBM_SPEC],
        [VMEM_SPEC] * count,
        [pltpu.SemaphoreType.DMA((2 * count,))],
        2,
        vmem,
    )(plan, x)


def unpack_kernel(layout, *refs):
    pieces, out_ref, held, in_sem, out_sem = refs[:-4], *refs[-4:]
    width = 2 * BLK
    loads, stores = [], []
    for i, piece in enumerate(pieces):
        start = pl.multiple_of(layout.pair_at(*divmod(i, layout.team)) * width, width)
        loads.append(pltpu.make_async_copy(piece, held.at[i], in_sem.at[i]))
        stores.append(
            pltpu.make_async_copy(held.at[i], out_ref.at[:, pl.ds(start, width)], out_sem.at[i])
        )
    for load in loads:
        load.start()
    for load, store in zip(loads, stores):
        load.wait()
        store.start()
    for store in stores:
        store.wait()


def unpack(layout, pieces):
    rows, width = pieces[0].shape
    count = len(pieces)
    return call(
        functools.partial(unpack_kernel, layout),
        "unpack",
        f32(rows, count * width),
        [HBM_SPEC] * count,
        HBM_SPEC,
        [
            pltpu.VMEM((count, rows, width), jnp.float32),
            pltpu.SemaphoreType.DMA((count,)),
            pltpu.SemaphoreType.DMA((count,)),
        ],
        3,
    )(*pieces)


def gather_terms_kernel(layout, *refs):
    pieces, (blocks_ref, terms_ref) = refs[:-2], refs[-2:]
    rows = pieces[0].shape[0]
    for i, piece in enumerate(pieces):
        at = pl.ds(pl.multiple_of(layout.partner(i) * rows, rows), rows)
        blocks_ref[0, at, :] = piece[:, :BLK]
        blocks_ref[1, at, :] = piece[:, BLK:]
    pair_terms(blocks_ref, terms_ref)


def gather_terms(layout, pieces):
    tokens = pieces[0].shape[0] * len(pieces)
    return call(
        functools.partial(gather_terms_kernel, layout),
        "gather_terms",
        [f32(2, tokens, BLK), f32(BLK + SQUARES, BLK)],
        [VMEM_SPEC] * len(pieces),
        [VMEM_SPEC] * 2,
        [],
        2,
    )(*pieces)


def choose_terms_kernel(pick_upper, pick_lower, uppers, lowers, *refs):
    inputs, (blocks_ref, terms_ref) = refs[:-2], refs[-2:]

    def fetch(m, at):
        rows = inputs[at[0]].shape[0]
        for i, place in enumerate(at):
            blocks_ref[m, i * rows : (i + 1) * rows, :] = inputs[place][...]

    for m, (pick, choices) in enumerate(((pick_upper, uppers), (pick_lower, lowers))):
        chosen = pick()
        pl.when(chosen)(functools.partial(fetch, m, choices[0]))
        pl.when(jnp.logical_not(chosen))(functools.partial(fetch, m, choices[1]))
    pair_terms(blocks_ref, terms_ref)


def choose_terms(picks, uppers, lowers):
    tokens = sum(part.shape[0] for part in uppers[0])
    inputs, places = [], []
    for choice in (*uppers, *lowers):
        places.append(tuple(range(len(inputs), len(inputs) + len(choice))))
        inputs.extend(choice)
    return call(
        functools.partial(choose_terms_kernel, *picks, places[:2], places[2:]),
        "choose_terms",
        [f32(2, tokens, BLK), f32(BLK + SQUARES, BLK)],
        [VMEM_SPEC] * len(inputs),
        [VMEM_SPEC] * 2,
        [],
        2,
    )(*inputs)


def edge_terms_kernel(layout, pair_ref, inv_ref, old_blocks_ref, old_terms_ref, blocks_ref, terms_ref):
    chunk = min(CHUNK, pair_ref.shape[1])
    blocks_ref[...] = old_blocks_ref[...]

    def step(i, _):
        rows = pl.ds(pl.multiple_of(i * chunk, chunk), chunk)
        blocks_ref[1, rows, :] = turned(pair_ref[0, rows, :], pair_ref[1, rows, :], inv_ref, 0)
        return 0

    @pl.when(layout.final())
    def _():
        lax.fori_loop(0, pair_ref.shape[1] // chunk, step, 0)
        pair_terms(blocks_ref, terms_ref)

    @pl.when(jnp.logical_not(layout.final()))
    def _():
        terms_ref[...] = old_terms_ref[...]


def edge_terms(layout, pair, factors, blocks, terms):
    return call(
        functools.partial(edge_terms_kernel, layout),
        "edge_terms",
        [f32(*blocks.shape), f32(*terms.shape)],
        [VMEM_SPEC] * 4,
        [VMEM_SPEC] * 2,
        [],
        1,
    )(pair, factors, blocks, terms)


def total_terms(refs):
    total = refs[0][...]
    for ref in refs[1:]:
        total = total + ref[...]
    return total


def start_factor(terms, corr_ref, work_ref):
    square = (BLK, BLK)
    diagonal = iota2(square, 0) == iota2(square, 1)
    ident = jnp.where(diagonal, 1.0, 0.0).astype(jnp.float32)
    upper_sq, lower_sq = terms[BLK : BLK + 1], terms[BLK + 1 : BLK + 2]
    upper_sq = jnp.sum(
        jnp.where(diagonal, jnp.broadcast_to(upper_sq, square), 0.0), axis=1, keepdims=True
    )
    corr = terms[:BLK] * lax.rsqrt(upper_sq + epsilon) * lax.rsqrt(lower_sq + epsilon)
    corr_ref[0] = corr
    corr_ref[1] = -jnp.transpose(corr)
    for m in range(2):
        whole = ident + contract(corr_ref[m], corr_ref[m], 1, 1)
        for r in range(2):
            for c in range(2):
                work_ref[m, r, c] = whole[HALF * r : HALF * (r + 1), HALF * c : HALF * (c + 1)]


def finish_factor(corr_ref, work_ref, inv_ref):
    for m in range(2):
        whole = jnp.concatenate(
            [jnp.concatenate([work_ref[m, r, 0], work_ref[m, r, 1]], axis=1) for r in range(2)],
            axis=0,
        )
        inv_ref[m, :, :BLK] = whole
        inv_ref[m, :, BLK:] = contract(whole, corr_ref[m], 1, 0)


CORR_SHAPE = (2, BLK, BLK)
WORK_SHAPE = (2, 2, 2, HALF, HALF)


def factor_kernel(*refs):
    terms, (inv_ref, corr_ref, work_ref) = refs[:-3], refs[-3:]
    start_factor(total_terms(terms), corr_ref, work_ref)

    def step(h, _):
        half_step(work_ref, h)
        return 0

    lax.fori_loop(0, 2, step, 0)
    finish_factor(corr_ref, work_ref, inv_ref)


def factor(terms):
    return call(
        factor_kernel,
        "factor",
        f32(2, BLK, 2 * BLK),
        [VMEM_SPEC] * len(terms),
        VMEM_SPEC,
        [pltpu.VMEM(CORR_SHAPE, jnp.float32), pltpu.VMEM(WORK_SHAPE, jnp.float32)],
        11,
    )(*terms)


def factor_start_kernel(*refs):
    terms, (corr_ref, work_ref) = refs[:-2], refs[-2:]
    start_factor(total_terms(terms), corr_ref, work_ref)
    half_step(work_ref, 0)


def factor_start(terms):
    return call(
        factor_start_kernel,
        "factor_start",
        [f32(*CORR_SHAPE), f32(*WORK_SHAPE)],
        [VMEM_SPEC] * len(terms),
        [VMEM_SPEC] * 2,
        [],
        6,
    )(*terms)


def factor_finish_kernel(corr_ref, held_ref, inv_ref, work_ref):
    work_ref[...] = held_ref[...]
    half_step(work_ref, 1)
    finish_factor(corr_ref, work_ref, inv_ref)


def factor_finish(corr, work):
    return call(
        factor_finish_kernel,
        "factor_finish",
        f32(2, BLK, 2 * BLK),
        [VMEM_SPEC] * 2,
        VMEM_SPEC,
        [pltpu.VMEM(WORK_SHAPE, jnp.float32)],
        5,
    )(corr, work)


def turned(own, other, inv_ref, m):
    return contract(own, inv_ref[m, :, :BLK], 1, 1) + contract(other, inv_ref[m, :, BLK:], 1, 1)


def turn_kernel(m, blocks_ref, inv_ref, *out_refs):
    chunk = min(CHUNK, out_refs[0].shape[0])
    for part, out_ref in enumerate(out_refs):
        first = part * out_ref.shape[0]

        def step(i, _):
            start = pl.multiple_of(i * chunk, chunk)
            at = pl.ds(first + start, chunk)
            out_ref[pl.ds(start, chunk), :] = turned(
                blocks_ref[m, at, :], blocks_ref[1 - m, at, :], inv_ref, m
            )
            return 0

        lax.fori_loop(0, out_ref.shape[0] // chunk, step, 0)


def turn(m, blocks, factors, parts=1):
    out = call(
        functools.partial(turn_kernel, m),
        "turn",
        [f32(blocks.shape[1] // parts, BLK)] * parts,
        [VMEM_SPEC] * 2,
        [VMEM_SPEC] * parts,
        [],
        2,
    )(blocks, factors)
    return list(out)


def turn_out_kernel(layout, partners, blocks_ref, inv_ref, *refs):
    outs, out_ref = refs[:-1], refs[-1]
    rows = outs[0].shape[0]
    spans = [pl.ds(pl.multiple_of(layout.partner(i) * rows, rows), rows) for i in partners]

    def step(m, _):
        own = jnp.concatenate([blocks_ref[m, at, :] for at in spans], axis=0)
        other = jnp.concatenate([blocks_ref[1 - m, at, :] for at in spans], axis=0)
        out_ref[m] = turned(own, other, inv_ref, m)
        return 0

    lax.fori_loop(0, 2, step, 0)
    for i, out in enumerate(outs):
        out[:, :BLK] = out_ref[0, i * rows : (i + 1) * rows, :]
        out[:, BLK:] = out_ref[1, i * rows : (i + 1) * rows, :]


def turn_out(layout, partners, blocks, factors):
    rows = blocks.shape[1] // layout.team
    count = len(partners)
    return call(
        functools.partial(turn_out_kernel, layout, partners),
        "turn_out",
        [f32(rows, 2 * BLK)] * count,
        [VMEM_SPEC] * 2,
        [VMEM_SPEC] * count,
        [pltpu.VMEM((2, rows * count, BLK), jnp.float32)],
        2,
    )(blocks, factors)


def on_device(activations, plan):
    token_axes = ("rows", "sub")
    all_axes = ("rows", "cols", "sub")
    layout = Layout(activations.shape[1] // BLK)
    team, teams, held = layout.team, layout.teams, layout.held
    subs, columns, token_group = layout.subs, layout.columns, layout.token_group

    def exchange(pieces):
        arrived = [pieces[0]]
        for shift, piece in zip(layout.shifts[1:], pieces[1:]):
            route = [(t, t ^ shift) for t in range(token_group)]
            arrived.append(lax.ppermute(piece, token_axes, route))
        return arrived

    def position(at, group):
        home, inner = divmod(at, team)
        inner = team - 1 - inner if home % 2 else inner
        row, sub = divmod(group * team + inner, subs)
        return (row * columns + home) * subs + sub

    def shared(terms, places=range(columns * team)):
        gathered = []
        for step in range(1, teams):
            route = [
                (position(at, group), position(at, (group + step) % teams))
                for at in places
                for group in range(teams)
            ]
            gathered.append(lax.ppermute(terms, all_axes, route))
        return gathered

    def along(block, distance):
        route = []
        for at in range(columns * team):
            if 0 <= at + distance < columns * team:
                for group in range(teams):
                    route.append((position(at, group), position(at + distance, group)))
        return lax.ppermute(block, all_axes, route)

    def always():
        return lax.axis_index("cols") >= 0

    early = [(0, i) for i in range(1, team)]
    late = [(0, 0)] + [(g, i) for g in range(1, held) for i in range(team)]
    packed = list(pack(layout, early, plan, activations, PACK_VMEM_LIMIT))
    plan, packed[0] = lax.optimization_barrier((plan, packed[0]))
    pieces = dict(zip(early, packed))
    pieces.update(zip(late, pack(layout, late, plan, activations, VMEM_LIMIT)))
    arrived = []
    for g in range(held):
        piece = [pieces[g, i] for i in range(team)]
        if arrived:
            piece, arrived[-1] = lax.optimization_barrier((piece, arrived[-1]))
        arrived.append(exchange(piece))
    ready = [gather_terms(layout, piece) for piece in arrived]
    summed = [[terms] + shared(terms) for _, terms in ready]
    top = held - 1

    def next_blocks(g, uppers, lowers, edge, leaving, arriving):
        if g == 0:
            from_above, pick_upper = (uppers[0], arriving), layout.first
        elif g == 1:
            from_above, pick_upper = (lowers[0], uppers[0]), layout.first
        else:
            from_above, pick_upper = (uppers[g - 1],) * 2, always
        if g == top:
            from_below, pick_lower = (edge, leaving), layout.final
        else:
            from_below, pick_lower = (lowers[g + 1],) * 2, always
        return choose_terms((pick_upper, pick_lower), from_above, from_below)

    for g in range(1, held):
        summed[0][0], summed[g][0] = lax.optimization_barrier((summed[0][0], summed[g][0]))
    uppers, lowers, nexts = [None] * held, [None] * held, [None] * held
    leaving = None
    for g in range(top):
        factors = factor(summed[g])
        lowers[g] = turn(1, ready[g][0], factors)
        if g == 0:
            leaving = [along(part, -1) for part in lowers[0]]
        uppers[g] = turn(0, ready[g][0], factors)
    if top:
        corr, work = factor_start(summed[top])
        work, leaving = lax.optimization_barrier((work, leaving))
        blocks, terms = next_blocks(top, uppers, lowers, leaving, leaving, None)
        end = columns * team - 1
        early = shared(terms, range(end))
        work, terms = lax.optimization_barrier((work, terms))
        factors = factor_finish(corr, work)
        blocks, terms = edge_terms(layout, ready[top][0], factors, blocks, terms)
        late = shared(terms, [end])
        nexts[top] = (blocks, [terms] + early + late)
        factors, terms = lax.optimization_barrier((factors, terms))
        uppers[top] = turn(0, ready[top][0], factors, UP_PARTS)
        arriving = [along(part, 1) for part in uppers[top]]
        lowers[top] = turn(1, ready[top][0], factors)
        for term in early + late:
            lowers[top][0], term = lax.optimization_barrier((lowers[top][0], term))
    else:
        factors = factor(summed[0])
        uppers[0] = turn(0, ready[0][0], factors, UP_PARTS)
        lowers[0] = turn(1, ready[0][0], factors, UP_PARTS)
        arriving = [
            along(jnp.where(layout.first(), low, up), 1) for low, up in zip(lowers[0], uppers[0])
        ]
        leaving = [along(part, -1) for part in lowers[0]]
    for g in reversed(range(held)):
        if nexts[g] is None:
            blocks, terms = next_blocks(g, uppers, lowers, uppers[top], leaving, arriving)
            nexts[g] = (blocks, [terms] + shared(terms))

    for g in range(1, held):
        nexts[0][1][0], nexts[g][1][0] = lax.optimization_barrier((nexts[0][1][0], nexts[g][1][0]))
    far = [i for i, shift in enumerate(layout.shifts) if shift >= subs]
    near = [i for i, shift in enumerate(layout.shifts) if shift < subs]
    results = [None] * held
    for g in reversed(range(held)):
        blocks, terms = nexts[g]
        factors = factor(terms)
        sent = [None] * team
        for partners in (far, near):
            if partners:
                for i, piece in zip(partners, turn_out(layout, partners, blocks, factors)):
                    sent[i] = piece
        results[g] = exchange(sent)
    return unpack(layout, [piece for result in results for piece in result])


def solution(mesh):
    in_specs = (P(("groups", "rows", "sub"), "cols"), P())
    out_specs = P(("groups", "rows", "sub"), "cols")
    return jax.shard_map(
        on_device, mesh=mesh, in_specs=in_specs, out_specs=out_specs, check_vma=False
    )
```
